256 devices in a mesh: rep: 16 (over x_lo, z), fsdp: 16 (over x_hi, y, core).
Axes of the slice: x: 4 (x_hi: 2, x_lo: 2; x = x_hi * 2 + x_lo), y: 4, z: 8, core: 2. Of those that a mesh axis runs over, the one named last changes fastest.
Arguments:
- params: float32 [16, 4096, 1376], P('rep', 'fsdp'), may hold values from -0.09375 to 0.09375
- first_moment: float32 [16, 4096, 1376], P('rep', 'fsdp'), may hold values from -4 to 4
- second_moment: float32 [16, 4096, 1376], P('rep', 'fsdp'), may hold values from 0.01 to 1
- push_weight: float32 [16], P('rep'), may hold values from 0.5 to 2
- tokens: bfloat16 [16, 4096, 4096], P('rep', 'fsdp'), may hold values from -6 to 6
- cotangent: bfloat16 [16, 4096, 1376], P('rep', 'fsdp'), may hold values from -0.1875 to 0.1875
- step: int32 [], replicated, may hold values from 0 to 3999
Outputs:
- new_params: float32 [16, 4096, 1376], P('rep', 'fsdp')
- new_first: float32 [16, 4096, 1376], P('rep', 'fsdp')
- new_second: float32 [16, 4096, 1376], P('rep', 'fsdp')
- new_weight: float32 [16], P('rep')
The draws below stay inside these ranges and needn't reach their ends.
All inputs are finite; a program needn't handle non-finite values.
Results may differ from the reference program's by a relative error of at most 0.008.
Values may be sent and summed in bfloat16 or wider, within the bound.
No kernel may reach another device: no remote copies, remote signals or barrier semaphores. Data moves between devices by JAX's collectives and lax.ppermute only.
A program may use at most 128 MiB of HBM per device.

```python
import math
import jax
import jax.numpy as jnp
from jax import lax

D = 4096
FF = 1376
TOK_DEV = 256
TOKENS = 4096
REPS = 16
N_REP = 16
N_FSDP = 16


def with_spikes(values, rng, source, target, parts, factor):
    def block_of(axis_at):
        return (jnp.arange(values.shape[axis_at]) // (values.shape[axis_at] // parts)).reshape((-1,) + (1,) * (values.ndim - 1 - axis_at))

    first = jax.random.permutation(rng, parts)[block_of(target)]
    second = (block_of(target) + parts // 2) % parts
    return jnp.where((block_of(source) == first) | (block_of(source) == second), factor * values, values)


def steps_of(key, extent, split, smallest, high):
    def one(position, parts):
        heights = jax.random.uniform(jax.random.fold_in(jax.random.fold_in(key, 6), position), (parts,), jnp.float32, smallest / len(split), high / len(split))
        return jnp.repeat(jnp.exp(heights), extent[position] // parts).reshape((-1,) + (1,) * (len(extent) - position - 1))

    factor_of = one(*split[0])
    for cut in split[1:]:
        factor_of = factor_of * one(*cut)
    return factor_of


def noise(key, shape, spread, most, split=(), dtype=jnp.bfloat16):
    values = jax.random.normal(key, shape, jnp.float32) * spread
    if len(split) > 0:
        values = steps_of(key, shape, split, -0.22, 0.18) * values
    return jnp.clip(values, min=-most, max=most).astype(dtype)


def bell_draw_with(own_key, dims, scale, limit, shards, heavy, dtype=jnp.bfloat16):
    values = scale * jax.random.normal(own_key, dims, jnp.float32)
    if shards:
        values = values * steps_of(own_key, dims, shards, -0.22, 0.18)
    return jnp.clip(with_spikes(values, jax.random.fold_in(own_key, 3), *heavy), -limit, limit).astype(dtype)


def setup_inputs(seed: int = 0) -> dict:
    keys = jax.random.split(jax.random.key(seed), 8)
    params = noise(keys[0], (REPS, D, FF), D ** -0.5, 0.09375, ((0, 16), (1, 16)), jnp.float32)
    first_moment = noise(keys[1], (REPS, D, FF), 0.3, 4.0, ((0, 16), (1, 16)), jnp.float32)
    second_moment = jnp.clip(jnp.exp(math.log(1.0) - 4.6051702 * jax.random.uniform(keys[2], (REPS, D, FF), jnp.float32) ** steps_of(keys[2], (REPS, D, FF), ((0, 16), (1, 16)), -0.2, 0.2)), 0.01, 1.0)
    push_weight = jnp.clip(jnp.exp(math.log(2.0) - 1.3862944 * jax.random.uniform(keys[3], (REPS,), jnp.float32) ** steps_of(keys[3], (REPS,), ((0, 16),), -0.2, 0.2)), 0.5, 2.0)
    tokens = bell_draw_with(keys[4], (REPS, TOKENS, D), 1.0, 6.0, ((0, 16), (1, 16)), (1, 2, 16, 2.0))
    cotangent = noise(keys[5], (REPS, TOKENS, FF), (TOKENS // 4) ** -0.5, 0.1875, ((0, 16), (1, 16)))
    step = jax.random.randint(keys[6], (), 0, 4000).astype(jnp.int32)
    return dict(params=params, first_moment=first_moment, second_moment=second_moment, push_weight=push_weight, tokens=tokens, cotangent=cotangent, step=step)


def replica_grad(tok, weights, cot):
    gate = jnp.dot(tok, weights, preferred_element_type=jnp.float32)
    sig = jax.nn.sigmoid(gate)
    slope = (cot.astype(jnp.float32) * sig * (1.0 + gate * (1.0 - sig))).astype(jnp.bfloat16)
    tok_blocks = tok.reshape(N_FSDP, TOK_DEV, D)
    slope_blocks = slope.reshape(N_FSDP, TOK_DEV, FF)

    def add_block(total, pair):
        piece = jnp.dot(pair[0].T, pair[1], preferred_element_type=jnp.float32)
        rounded = lax.optimization_barrier(piece.astype(jnp.bfloat16))
        return (total + rounded.astype(jnp.float32), None)
    grad, unused = lax.scan(add_block, jnp.zeros((D, FF), jnp.float32), (tok_blocks, slope_blocks))
    return grad

def reference(params, first_moment, second_moment, push_weight, tokens, cotangent, step):
    stepf = step.astype(jnp.float32) + 1.0
    rate = 0.01 * jnp.minimum(1.0, stepf / 2000.0)
    corr_one = 1.0 - jnp.exp(stepf * jnp.log(jnp.float32(0.9)))
    corr_two = 1.0 - jnp.exp(stepf * jnp.log(jnp.float32(0.999)))

    def one(items):
        master, first, second, weight_now, tok, cot = items
        weights = (master / weight_now).astype(jnp.bfloat16)
        grad = replica_grad(tok, weights, cot)
        first_new = 0.9 * first + 0.1 * grad
        second_new = 0.999 * second + 0.001 * grad * grad
        update = first_new / corr_one / (jnp.sqrt(second_new / corr_two) + 1e-08)
        moved = master - rate * (update + 0.1 * master)
        return (moved, first_new, second_new)
    moved, new_first, new_second = lax.map(one, (params, first_moment, second_moment, push_weight, tokens, cotangent))
    log_rep = N_REP.bit_length() - 1
    offset = jnp.left_shift(jnp.int32(1), (step % log_rep).astype(jnp.int32))
    new_params = 0.5 * (moved + jnp.roll(moved, offset, axis=0))
    new_weight = 0.5 * (push_weight + jnp.roll(push_weight, offset, axis=0))
    return (new_params, new_first, new_second, new_weight)
```

```python
from functools import partial

import jax
import jax.numpy as jnp
import numpy as np
from jax import lax
from jax.experimental import pallas as pl
from jax.experimental.pallas import tpu as pltpu
from jax.sharding import PartitionSpec as P

ANY = pl.BlockSpec(memory_space=pl.ANY)
VMEM = pl.BlockSpec(memory_space=pltpu.VMEM)
SMEM = pl.BlockSpec(memory_space=pltpu.SMEM)
BF = jnp.bfloat16
F32 = jnp.float32
PARAMS = pltpu.CompilerParams(vmem_limit_bytes=40 * 1024 * 1024)

D = 4096
FF = 1376
HALF = FF // 2
ROWS = 256
CHUNKS = ((0, 352), (352, 336))

STAGES = ([(0, 0), (0, -1), (0, 1), (1, 0)], [(0, 2), (1, -1), (1, 1)], [(1, 2)])
PARTS = ([(1, 2), (1, 1), (1, -1)], [(0, 2), (0, 1), (0, -1), (1, 0), (0, 0)])


def route(move):
    pairs = []
    for f in range(16):
        x, y, c = move(f // 8, f // 2 % 4, f % 2)
        pairs.append((f, x % 2 * 8 + y % 4 * 2 + c % 2))
    return pairs


CORE = route(lambda x, y, c: (x, y, c + 1))
UP = route(lambda x, y, c: (x, y + 1, c))
DOWN = route(lambda x, y, c: (x, y - 1, c))
ACROSS = route(lambda x, y, c: (x + 1, y, c))


WAYS = {"core": CORE, "up": UP, "down": DOWN, "across": ACROSS}


def move(block, way):
    return lax.ppermute(block, "fsdp", way)


class Links:
    def __init__(self):
        self.sent = {}

    def move(self, block, link, name):
        earlier = self.sent.setdefault(link, [])
        if len(earlier) >= 2:
            block = lax.optimization_barrier((block, earlier[-2]))[0]
        with jax.named_scope(name):
            earlier.append(move(block, WAYS[link]))
        return earlier[-1]


def chip(f, piece):
    dx, dy = piece
    return ((f // 8 + dx) & 1) * 4 + ((f // 2 + dy) & 3)


def cast_kernel(f_ref, weight_ref, params_ref, mine_ref, other_ref):
    c = f_ref[0] & 1
    weight = weight_ref[0]
    for out, half in ((other_ref, 1 - c), (mine_ref, c)):

        def body(i, carry):
            src = pl.ds(pl.multiple_of(half * HALF + i * 16, 16), 16)
            dst = pl.ds(pl.multiple_of(i * 16, 16), 16)
            out[dst, :] = (params_ref[src, :] / weight).astype(BF)
            return carry

        lax.fori_loop(0, HALF // 16, body, 0)


def token_copies(f, pieces, own_ref, oth_ref, buf, sems):
    copies = []
    for i, piece in enumerate(pieces):
        cols = pl.ds(pl.multiple_of(chip(f, piece) * 2 * ROWS, 2 * ROWS), 2 * ROWS)
        copies.append(
            (
                pltpu.make_async_copy(own_ref.at[:, cols], buf.at[i, pl.ds(0, ROWS)], sems.at[i, 0]),
                pltpu.make_async_copy(oth_ref.at[:, cols], buf.at[i, pl.ds(ROWS, ROWS)], sems.at[i, 1]),
            )
        )
    return copies


def gate_sum(f, pieces, own_ref, oth_ref, weights, tok, wbuf, sems, start_ref, out_ref):
    c = f & 1
    copies = token_copies(f, pieces, own_ref, oth_ref, tok, sems)
    for i in range(len(pieces)):
        blocks = ()
        for ab in range(2):
            cols = pl.ds(pl.multiple_of((c ^ ab) * ROWS, ROWS), ROWS)
            blocks += (
                pltpu.make_async_copy(weights[2 * i + ab], wbuf.at[i, :, cols], sems.at[i, 2 + ab]),
            )
        copies[i] += blocks
    for group in copies:
        for copy in group:
            copy.start()
    for i, group in enumerate(copies):
        for copy in group:
            copy.wait()
        term = lax.dot_general(
            wbuf[i], tok[i], (((1,), (1,)), ((), ())), preferred_element_type=F32
        )
        if i > 0:
            out_ref[...] += term
        elif start_ref is None:
            out_ref[...] = term
        else:
            out_ref[...] = start_ref[...] + term


def first_kernel(f_ref, own_ref, oth_ref, *refs):
    weights, (out_ref, tok, wbuf, sems) = refs[:8], refs[8:]
    gate_sum(f_ref[0], STAGES[0], own_ref, oth_ref, weights, tok, wbuf, sems, None, out_ref)


def next_kernel(f_ref, own_ref, oth_ref, sum_ref, *refs):
    weights, (out_ref, tok, wbuf, sems) = refs[:6], refs[6:]
    gate_sum(f_ref[0], STAGES[1], own_ref, oth_ref, weights, tok, wbuf, sems, sum_ref, out_ref)


def last_kernel(f_ref, own_ref, oth_ref, sum_ref, cot_ref, cot_oth_ref, *refs):
    weights, (out_ref, tok, wbuf, sems, gate, cot, cot_sem) = refs[:2], refs[2:]
    f = f_ref[0]
    rows = pl.ds(pl.multiple_of((f & 1) * HALF, 16), HALF)
    cot_copy = pltpu.make_async_copy(cot_ref.at[rows, :], cot, cot_sem)
    cot_copy.start()
    gate_sum(f, STAGES[2], own_ref, oth_ref, weights, tok, wbuf, sems, sum_ref, gate)
    cot_copy.wait()

    def body(i, carry):
        rows = pl.ds(pl.multiple_of(i * 16, 16), 16)
        for half, part in ((0, cot), (1, cot_oth_ref)):
            cols = slice(half * ROWS, half * ROWS + ROWS)
            g = gate[rows, cols]
            sig = 1.0 / (1.0 + jnp.exp(-g))
            out_ref[rows, cols] = (
                part[rows, :].astype(F32) * sig * (1.0 + g * (1.0 - sig))
            ).astype(BF)
        return carry

    lax.fori_loop(0, HALF // 16, body, 0)


def grad_kernel(pieces, f_ref, own_ref, oth_ref, slope_ref, *refs):
    n = len(pieces)
    outs, (tok, res, sems, out_sems) = refs[: 2 * n], refs[2 * n :]
    f = f_ref[0]
    c = f & 1
    copies = token_copies(f, pieces, own_ref, oth_ref, tok, sems)
    for pair in copies:
        for copy in pair:
            copy.start()

    def write(i, k):
        lo, size = CHUNKS[k]
        return pltpu.make_async_copy(
            res.at[i, :, pl.ds(lo, size)], outs[2 * i + k], out_sems.at[i, k]
        )

    def body(i, carry):
        for copy in (
            pltpu.make_async_copy(own_ref.at[:, pl.ds(0, 2 * ROWS)], tok.at[i, pl.ds(0, ROWS)], sems.at[i, 0]),
            pltpu.make_async_copy(oth_ref.at[:, pl.ds(0, 2 * ROWS)], tok.at[i, pl.ds(ROWS, ROWS)], sems.at[i, 1]),
        ):
            copy.wait()
        both = jnp.dot(slope_ref[...], tok[i], preferred_element_type=F32).astype(BF)
        for core in range(2):
            res[i, c ^ core] = both[:, core * ROWS : core * ROWS + ROWS]
        for j in range(n):

            @pl.when(i == j)
            def _():
                write(j, 0).start()
                write(j, 1).start()

        return carry

    lax.fori_loop(0, n, body, 0)
    for i in range(n):
        write(i, 0).wait()
        write(i, 1).wait()


LOG_ONE = np.log(np.float32(0.9))
LOG_TWO = np.log(np.float32(0.999))


def adam_kernel(lo, size, has_prev, f_ref, step_ref, params_ref, first_ref, second_ref, *refs):
    refs = refs[2:] if has_prev else refs
    base, low, high, crossed, swapped = refs[:5]
    moved_ref, sent_ref, first_out, second_out = refs[5:9]
    pbuf, mbuf, vbuf, in_sems, out_sems = refs[9:]
    c = f_ref[0] & 1

    def rows(i):
        half = c if i == 0 else 1 - c
        return pl.ds(pl.multiple_of(half * HALF + lo, 16), size)

    loads = []
    for i in range(2):
        for j, (src, buf) in enumerate(((first_ref, mbuf), (second_ref, vbuf), (params_ref, pbuf))):
            copy = pltpu.make_async_copy(src.at[rows(i), :], buf.at[i], in_sems.at[i, j])
            copy.start()
            loads.append(copy)
    stepf = jnp.full((1, ROWS), step_ref[0], jnp.int32).astype(F32) + 1.0
    rate = 0.01 * jnp.minimum(1.0, stepf / 2000.0)
    corr_one = 1.0 / (1.0 - jnp.exp(stepf * LOG_ONE))
    corr_two = 1.0 / (1.0 - jnp.exp(stepf * LOG_TWO))
    for copy in loads:
        copy.wait()

    def body(t, carry):
        at = pl.ds(pl.multiple_of(t * 16, 16), 16)
        for i in range(2):
            if i == 0:
                grad = base[0, at].astype(F32) + low[at].astype(F32)
                grad = grad + high[at].astype(F32) + crossed[0, at].astype(F32)
            else:
                grad = swapped[at].astype(F32)
            new_first = 0.9 * mbuf[i, at] + 0.1 * grad
            new_second = 0.999 * vbuf[i, at] + 0.001 * grad * grad
            mbuf[i, at] = new_first
            vbuf[i, at] = new_second
            master = pbuf[i, at]
            update = new_first * corr_one / (jnp.sqrt(new_second * corr_two) + 1e-08)
            moved = master - rate * (update + 0.1 * master)
            moved_ref[i, at] = 0.5 * moved
            sent_ref[i, at] = moved.astype(BF)
        return carry

    lax.fori_loop(0, size // 16, body, 0)
    stores = []
    for i in range(2):
        for j, (buf, dst) in enumerate(((mbuf, first_out), (vbuf, second_out))):
            copy = pltpu.make_async_copy(buf.at[i], dst.at[rows(i), :], out_sems.at[i, j])
            copy.start()
            stores.append(copy)
    for copy in stores:
        copy.wait()


def mix_kernel(lo, size, has_prev, f_ref, moved_ref, arrived_ref, *refs):
    out_ref, buf, sems = refs[1:] if has_prev else refs
    c = f_ref[0] & 1

    def body(t, carry):
        at = pl.ds(pl.multiple_of(t * 16, 16), 16)
        for i in range(2):
            buf[i, at] = moved_ref[i, at] + 0.5 * arrived_ref[i, at].astype(F32)
        return carry

    lax.fori_loop(0, size // 16, body, 0)
    stores = []
    for i in range(2):
        half = c if i == 0 else 1 - c
        rows = pl.ds(pl.multiple_of(half * HALF + lo, 16), size)
        copy = pltpu.make_async_copy(buf.at[i], out_ref.at[rows, :], sems.at[i])
        copy.start()
        stores.append(copy)
    for copy in stores:
        copy.wait()


def shape(*dims, dtype=BF):
    return jax.ShapeDtypeStruct(dims, dtype)


def added(*terms):
    total = terms[0].astype(F32)
    for term in terms[1:]:
        total = total + term.astype(F32)
    return total.astype(BF)


def gather(links, mine, other):
    a = mine
    b = links.move(other, "core", "B")
    have = {}
    low_a = links.move(a, "up", "upA")
    high_a = links.move(a, "down", "downA")
    over_a = links.move(a, "across", "acrossA")
    low_b = links.move(b, "up", "upB")
    high_b = links.move(b, "down", "downB")
    over_b = links.move(b, "across", "acrossB")
    two_a = links.move(low_a, "up", "up2A")
    over_high_a = links.move(over_a, "down", "downXA")
    over_low_a = links.move(over_a, "up", "upXA")
    two_b = links.move(high_b, "down", "down2B")
    over_low_b = links.move(over_b, "up", "upXB")
    over_high_b = links.move(over_b, "down", "downXB")
    over_two_a = links.move(two_a, "across", "across2A")
    over_two_b = links.move(two_b, "across", "across2B")
    return {
        (0, 0): (a, b),
        (0, -1): (low_a, low_b),
        (0, 1): (high_a, high_b),
        (0, 2): (two_a, two_b),
        (1, 0): (over_a, over_b),
        (1, -1): (over_low_a, over_low_b),
        (1, 1): (over_high_a, over_high_b),
        (1, 2): (over_two_a, over_two_b),
    }


def scattered(links, chunks):
    state = []
    for k, pieces in enumerate(chunks):
        tag = str(k)
        far = links.move(pieces[1, 2], "across", "far" + tag)
        cross_low = links.move(pieces[1, 1], "up", "upX" + tag)
        cross_high = links.move(pieces[1, -1], "down", "downX" + tag)
        crossed = links.move(added(pieces[1, 0], cross_low, cross_high), "across", "crossed" + tag)
        two = pieces[0, 2]
        if k == 0:
            up_b = links.move(pieces[0, 1][1], "up", "upB" + tag)
            down_a = links.move(pieces[0, -1][0], "down", "downA" + tag)
        via_a = links.move(added(two[0], far[0]), "up", "via_a" + tag)
        via_b = links.move(added(two[1], far[1]), "down", "via_b" + tag)
        if k > 0:
            up_b = links.move(pieces[0, 1][1], "up", "upB" + tag)
            down_a = links.move(pieces[0, -1][0], "down", "downA" + tag)
        state.append((pieces, crossed, up_b, down_a, via_a, via_b))
        if k > 0:
            yield finished(links, state[k - 1], str(k - 1))
    yield finished(links, state[-1], str(len(state) - 1))


def finished(links, state, tag):
    pieces, crossed, up_b, down_a, via_a, via_b = state
    up_a = links.move(added(pieces[0, 1][0], via_a), "up", "upA" + tag)
    down_b = links.move(added(pieces[0, -1][1], via_b), "down", "downB" + tag)
    base = pieces[0, 0]
    swapped = links.move(added(base[1], up_b, down_b, crossed[1]), "core", "swap" + tag)
    return (base, up_a, down_a, crossed), swapped


def grads(part, f, own, oth, slope):
    n = len(PARTS[part])
    out = pl.pallas_call(
        partial(grad_kernel, PARTS[part]),
        out_shape=[shape(2, size, ROWS) for _ in range(n) for lo, size in CHUNKS],
        in_specs=[SMEM, ANY, ANY, VMEM],
        out_specs=[ANY] * (2 * n),
        scratch_shapes=[
            pltpu.VMEM((n, 2 * ROWS, 2 * ROWS), BF),
            pltpu.VMEM((n, 2, HALF, ROWS), BF),
            pltpu.SemaphoreType.DMA((n, 2)),
            pltpu.SemaphoreType.DMA((n, 2)),
        ],
        compiler_params=PARAMS,
        cost_estimate=pl.CostEstimate(flops=n * HALF * 2**19, bytes_accessed=n * 2**20, transcendentals=0),
        name="grad",
    )(f, own, oth, slope)
    return [dict(zip(PARTS[part], out[k::2])) for k in range(2)]


def tail(offset, f, step, weight, params, first, second, own, oth, slope):
    routes = [((i - offset) % 16, i) for i in range(16)]
    weight_arrived = lax.ppermute(weight, "rep", routes)
    state = ()
    mixed = ()
    parts = [grads(part, f, own, oth, slope) for part in range(2)]
    sent = scattered(Links(), [{**parts[0][k], **parts[1][k]} for k in range(2)])
    out = []
    for (lo, size), (terms, swapped) in zip(CHUNKS, sent):
        base, up_a, down_a, crossed = terms
        prev = len(state)
        moved, short, *state = pl.pallas_call(
            partial(adam_kernel, lo, size, prev > 0),
            out_shape=[
                shape(2, size, ROWS, dtype=F32),
                shape(2, size, ROWS),
                shape(FF, ROWS, dtype=F32),
                shape(FF, ROWS, dtype=F32),
            ],
            in_specs=[SMEM, SMEM] + [ANY] * (3 + prev) + [VMEM] * 5,
            out_specs=[VMEM, VMEM, ANY, ANY],
            scratch_shapes=[pltpu.VMEM((2, size, ROWS), F32)] * 3
            + [pltpu.SemaphoreType.DMA((2, 3)), pltpu.SemaphoreType.DMA((2, 2))],
            input_output_aliases={5: 2, 6: 3} if prev else {},
            compiler_params=PARAMS,
            cost_estimate=pl.CostEstimate(
                flops=20 * size * 512, bytes_accessed=14 * size * 1024, transcendentals=0
            ),
            name="adam",
        )(f, step, params, first, second, *state, base, up_a, down_a, crossed, swapped)
        out.append((moved, lax.ppermute(short, "rep", routes)))
    for (lo, size), (moved, arrived) in zip(CHUNKS, out):
        prev = len(mixed)
        mixed = pl.pallas_call(
            partial(mix_kernel, lo, size, prev > 0),
            out_shape=[shape(FF, ROWS, dtype=F32)],
            in_specs=[SMEM, VMEM, VMEM] + [ANY] * prev,
            out_specs=[ANY],
            scratch_shapes=[
                pltpu.VMEM((2, size, ROWS), F32),
                pltpu.SemaphoreType.DMA((2,)),
            ],
            input_output_aliases={3: 0} if prev else {},
            compiler_params=PARAMS,
            name="mix",
        )(f, moved, arrived, *mixed)
    return mixed[0], state[0], state[1], 0.5 * (weight + weight_arrived)


def on_device(params, first, second, weight, tokens, cotangent, step):
    f = lax.axis_index("fsdp").astype(jnp.int32).reshape(1)
    step = step.reshape(1)
    params, first, second = (a[0].T for a in (params, first, second))
    own, cot = tokens[0], cotangent[0].T
    mine, other = pl.pallas_call(
        cast_kernel,
        out_shape=[shape(HALF, ROWS)] * 2,
        in_specs=[SMEM, SMEM, VMEM],
        out_specs=[VMEM, VMEM],
        compiler_params=PARAMS,
        name="cast",
    )(f, weight, params)
    links = Links()
    have = gather(links, mine, other)
    own_late = lax.optimization_barrier((own, have[0, 0][1]))[0]
    with jax.named_scope("tokens"):
        oth = move(own_late, CORE)
    cot_sent = lax.dynamic_slice(cot, ((1 - (f[0] & 1)) * HALF, 0), (HALF, ROWS))
    cot_sent = lax.optimization_barrier((cot_sent, oth))[0]
    with jax.named_scope("cotangent"):
        cot_oth = move(cot_sent, CORE)

    def stage(k, kernel, specs, *more, out=F32, extra=()):
        n = len(STAGES[k])
        return pl.pallas_call(
            kernel,
            out_shape=shape(HALF, 2 * ROWS, dtype=out),
            in_specs=[SMEM, ANY, ANY] + specs + [ANY] * (2 * n),
            out_specs=VMEM,
            scratch_shapes=[
                pltpu.VMEM((n, 2 * ROWS, 2 * ROWS), BF),
                pltpu.VMEM((n, HALF, 2 * ROWS), BF),
                pltpu.SemaphoreType.DMA((n, 4)),
            ]
            + list(extra),
            compiler_params=PARAMS,
            cost_estimate=pl.CostEstimate(
                flops=n * HALF * 2**19, bytes_accessed=n * 2**20, transcendentals=0
            ),
            name="gate" + str(k),
        )(f, own, oth, *more, *[w for p in STAGES[k] for w in have[p]])

    total = stage(0, first_kernel, [])
    total = stage(1, next_kernel, [VMEM], total)
    slope = stage(
        2, last_kernel, [VMEM, ANY, VMEM], total, cot, cot_oth, out=BF,
        extra=[
            pltpu.VMEM((HALF, 2 * ROWS), F32),
            pltpu.VMEM((HALF, ROWS), BF),
            pltpu.SemaphoreType.DMA,
        ],
    )
    mixed, new_first, new_second, new_weight = lax.switch(
        step[0] & 3,
        [partial(tail, 1 << bit) for bit in range(4)],
        f, step, weight, params, first, second, own, oth, slope,
    )
    return mixed.T[None], new_first.T[None], new_second.T[None], new_weight


def solution(mesh):
    block = P("rep", "fsdp", None)
    in_specs = (block, block, block, P("rep"), block, block, P())
    out_specs = (block, block, block, P("rep"))
    return jax.shard_map(
        on_device, mesh=mesh, in_specs=in_specs, out_specs=out_specs, check_vma=False
    )
```

```python
from functools import partial

import jax
import jax.numpy as jnp
import numpy as np
from jax import lax
from jax.experimental import pallas as pl
from jax.experimental.pallas import tpu as pltpu
from jax.sharding import PartitionSpec as P

ANY = pl.BlockSpec(memory_space=pl.ANY)
VMEM = pl.BlockSpec(memory_space=pltpu.VMEM)
SMEM = pl.BlockSpec(memory_space=pltpu.SMEM)
BF = jnp.bfloat16
F32 = jnp.float32
PARAMS = pltpu.CompilerParams(vmem_limit_bytes=16 * 1024 * 1024)

D = 4096
FF = 1376
HALF = FF // 2
ROWS = 256

STAGES = ([(0, 0), (0, -1), (0, 1)], [(1, 0), (0, 2)], [(1, -1), (1, 1), (1, 2)])
SOON = [(1, -1), (1, 1), (1, 2)]
LATER = [(0, 2), (0, 1), (0, -1), (1, 0), (0, 0)]


def route(move):
    pairs = []
    for f in range(16):
        x, y, c = move(f // 8, f // 2 % 4, f % 2)
        pairs.append((f, x % 2 * 8 + y % 4 * 2 + c % 2))
    return pairs


CORE = route(lambda x, y, c: (x, y, c + 1))
UP = route(lambda x, y, c: (x, y + 1, c))
DOWN = route(lambda x, y, c: (x, y - 1, c))
TWO = route(lambda x, y, c: (x, y + 2, c))
ACROSS = route(lambda x, y, c: (x + 1, y, c))


def move(block, way, name):
    with jax.named_scope(name):
        return lax.ppermute(block, "fsdp", way)


def after(block, *others):
    return lax.optimization_barrier((block, *others))[0]


def chip(f, piece):
    dx, dy = piece
    return ((f // 8 + dx) & 1) * 4 + ((f // 2 + dy) & 3)


def cast_kernel(f_ref, weight_ref, params_ref, mine_ref, other_ref):
    c = f_ref[0] & 1
    weight = weight_ref[0]
    for out, half in ((other_ref, 1 - c), (mine_ref.at[0], c)):
        rows = pl.ds(pl.multiple_of(half * HALF, 16), HALF)
        out[...] = (params_ref[rows, :] / weight).astype(BF)


def token_copies(f, pieces, own_ref, oth_ref, buf, sems):
    copies = []
    for i, piece in enumerate(pieces):
        cols = pl.ds(pl.multiple_of(chip(f, piece) * 2 * ROWS, 2 * ROWS), 2 * ROWS)
        copies.append(
            (
                pltpu.make_async_copy(own_ref.at[:, cols], buf.at[i, pl.ds(0, ROWS)], sems.at[i, 0]),
                pltpu.make_async_copy(oth_ref.at[:, cols], buf.at[i, pl.ds(ROWS, ROWS)], sems.at[i, 1]),
            )
        )
    return copies


def gate_sum(f, pieces, own_ref, oth_ref, weights, tok, wbuf, sems, start_ref, out_ref):
    c = f & 1
    copies = token_copies(f, pieces, own_ref, oth_ref, tok, sems)
    for i in range(len(pieces)):
        blocks = ()
        for ab in range(2):
            cols = pl.ds(pl.multiple_of((c ^ ab) * ROWS, ROWS), ROWS)
            blocks += (pltpu.make_async_copy(weights[i][ab], wbuf.at[i, :, cols], sems.at[i, 2 + ab]),)
        copies[i] += blocks
    for group in copies:
        for copy in group:
            copy.start()
    for i, group in enumerate(copies):
        for copy in group:
            copy.wait()
        term = lax.dot_general(
            wbuf[i], tok[i], (((1,), (1,)), ((), ())), preferred_element_type=F32
        )
        if i > 0:
            out_ref[...] += term
        elif start_ref is None:
            out_ref[...] = term
        else:
            out_ref[...] = start_ref[...] + term


def first_kernel(f_ref, own_ref, oth_ref, *refs):
    weights, (out_ref, tok, wbuf, sems) = [(r.at[0], r.at[1]) for r in refs[:3]], refs[3:]
    gate_sum(f_ref[0], STAGES[0], own_ref, oth_ref, weights, tok, wbuf, sems, None, out_ref)


def next_kernel(f_ref, own_ref, oth_ref, sum_ref, *refs):
    weights = [(refs[0].at[0], refs[0].at[1]), refs[1:3]]
    out_ref, tok, wbuf, sems = refs[3:]
    gate_sum(f_ref[0], STAGES[1], own_ref, oth_ref, weights, tok, wbuf, sems, sum_ref, out_ref)


def last_kernel(f_ref, own_ref, oth_ref, sum_ref, cot_ref, cot_oth_ref, *refs):
    weights = [(r.at[0], r.at[1]) for r in refs[:2]] + [refs[2:4]]
    slope_ref, *outs = refs[4:8]
    tok, wbuf, sems, gate, cot, cot_sem, res, out_sems = refs[8:]
    f = f_ref[0]
    c = f & 1
    rows = pl.ds(pl.multiple_of(c * HALF, 16), HALF)
    cot_copy = pltpu.make_async_copy(cot_ref.at[rows, :], cot, cot_sem)
    cot_copy.start()
    gate_sum(f, STAGES[2], own_ref, oth_ref, weights, tok, wbuf, sems, sum_ref, gate)
    cot_copy.wait()

    def body(i, carry):
        rows = pl.ds(pl.multiple_of(i * 16, 16), 16)
        for half, part in ((0, cot), (1, cot_oth_ref)):
            cols = slice(half * ROWS, half * ROWS + ROWS)
            g = gate[rows, cols]
            sig = 1.0 / (1.0 + jnp.exp(-g))
            slope_ref[rows, cols] = (
                part[rows, :].astype(F32) * sig * (1.0 + g * (1.0 - sig))
            ).astype(BF)
        return carry

    lax.fori_loop(0, HALF // 16, body, 0)
    grad_loop(c, slope_ref, tok, res, outs, out_sems, None)


def grad_loop(c, slope_ref, tok, res, outs, out_sems, arrival):
    def write(i):
        return pltpu.make_async_copy(res.at[i], outs[i], out_sems.at[i])

    def body(i, carry):
        if arrival is not None:
            arrival(i)
        both = jnp.dot(slope_ref[...], tok[i], preferred_element_type=F32).astype(BF)
        for core in range(2):
            res[i, c ^ core] = both[:, core * ROWS : core * ROWS + ROWS]
        for j in range(len(outs)):

            @pl.when(i == j)
            def _():
                write(j).start()

        return carry

    lax.fori_loop(0, len(outs), body, 0)
    for i in range(len(outs)):
        write(i).wait()


def grad_kernel(f_ref, own_ref, oth_ref, slope_ref, *refs):
    n = len(LATER)
    outs, (tok, res, sems, out_sems) = refs[:n], refs[n:]
    f = f_ref[0]
    for pair in token_copies(f, LATER, own_ref, oth_ref, tok, sems):
        for copy in pair:
            copy.start()

    def arrival(i):
        for j, src in enumerate((own_ref, oth_ref)):
            pltpu.make_async_copy(
                src.at[:, pl.ds(0, 2 * ROWS)], tok.at[i, pl.ds(j * ROWS, ROWS)], sems.at[i, j]
            ).wait()

    grad_loop(f & 1, slope_ref, tok, res, outs, out_sems, arrival)


LOG_ONE = np.log(np.float32(0.9))
LOG_TWO = np.log(np.float32(0.999))


def rows_of(c, i, t):
    half = c if i == 0 else 1 - c
    return pl.ds(pl.multiple_of(half * HALF + t * 16, 16), 16)


def total_kernel(base, up_a, up_b, down_a, down_b, crossed, kept_ref, sent_ref):
    def body(t, carry):
        at = pl.ds(pl.multiple_of(t * 16, 16), 16)
        for i, up, down in ((0, up_a, down_a), (1, up_b, down_b)):
            total = base[i, at].astype(F32) + up[at].astype(F32)
            total = total + down[at].astype(F32) + crossed[i, at].astype(F32)
            if i == 0:
                kept_ref[at] = total
            else:
                sent_ref[at] = total.astype(BF)
        return carry

    lax.fori_loop(0, HALF // 16, body, 0)


def grad_rows(kept, swapped, i, at):
    return kept[at] if i == 0 else swapped[at].astype(F32)


def step_kernel(
    f_ref, step_ref, params_ref, first_ref, second_ref, kept, swapped, moved_ref, sent_ref
):
    c = f_ref[0] & 1
    stepf = jnp.full((1, ROWS), step_ref[0], jnp.int32).astype(F32) + 1.0
    rate = 0.01 * jnp.minimum(1.0, stepf / 2000.0)
    corr_one = 1.0 / (1.0 - jnp.exp(stepf * LOG_ONE))
    corr_two = 1.0 / (1.0 - jnp.exp(stepf * LOG_TWO))

    def tile(t):
        at = pl.ds(pl.multiple_of(t * 16, 16), 16)
        done = []
        for i in range(2):
            rows = rows_of(c, i, t)
            grad = grad_rows(kept, swapped, i, at)
            new_first = 0.9 * first_ref[rows] + 0.1 * grad
            new_second = 0.999 * second_ref[rows] + 0.001 * grad * grad
            master = params_ref[rows]
            update = new_first * corr_one / (jnp.sqrt(new_second * corr_two) + 1e-08)
            done.append((i, at, master - rate * (update + 0.1 * master)))
        return done

    def store(done):
        for i, at, moved in done:
            moved_ref[i, at] = 0.5 * moved
            sent_ref[i, at] = moved.astype(BF)

    def body(t, carry):
        store(tile(3 * t) + tile(3 * t + 1) + tile(3 * t + 2))
        return carry

    lax.fori_loop(0, HALF // 48, body, 0)
    store(tile(HALF // 16 - 1))


def moment_kernel(f_ref, first_ref, second_ref, kept, swapped, first_out, second_out):
    c = f_ref[0] & 1

    def body(t, carry):
        at = pl.ds(pl.multiple_of(t * 16, 16), 16)
        for i in range(2):
            rows = rows_of(c, i, t)
            grad = grad_rows(kept, swapped, i, at)
            first_out[rows] = 0.9 * first_ref[rows] + 0.1 * grad
            second_out[rows] = 0.999 * second_ref[rows] + 0.001 * grad * grad
        return carry

    lax.fori_loop(0, HALF // 16, body, 0)


def mix_kernel(f_ref, moved_ref, arrived_ref, out_ref, buf, sems):
    c = f_ref[0] & 1
    copies = []
    for k, (lo, size) in enumerate(((0, 352), (352, 336))):
        for i in range(2):
            half = c if i == 0 else 1 - c
            rows = pl.ds(pl.multiple_of(half * HALF + lo, 16), size)
            copies.append(
                pltpu.make_async_copy(buf.at[i, pl.ds(lo, size)], out_ref.at[rows], sems.at[k, i])
            )

        def body(t, carry):
            at = pl.ds(pl.multiple_of(lo + t * 16, 16), 16)
            for i in range(2):
                buf[i, at] = moved_ref[i, at] + 0.5 * arrived_ref[i, at].astype(F32)
            return carry

        lax.fori_loop(0, size // 16, body, 0)
        for copy in copies[-2:]:
            copy.start()
    for copy in copies:
        copy.wait()


def shape(*dims, dtype=BF):
    return jax.ShapeDtypeStruct(dims, dtype)


def added(*terms):
    total = terms[0].astype(F32)
    for term in terms[1:]:
        total = total + term.astype(F32)
    return total.astype(BF)


def gather(mine, other, own, cot_sent):
    b = move(other, CORE, "B")
    oth = move(after(own, b), CORE, "tokens")
    both = lax.dynamic_update_slice(mine, b[None], (1, 0, 0))
    over = move(both, ACROSS, "across")
    low = move(both, UP, "up")
    high = move(both, DOWN, "down")
    two_a = move(low[0], UP, "twoA")
    two_b = move(high[1], DOWN, "twoB")
    cot_oth = move(after(cot_sent, oth), CORE, "cotangent")
    over_late = after(over, oth, cot_oth, two_a, two_b)
    over_low = move(over_late, UP, "upX")
    over_high = move(over_late, DOWN, "downX")
    over_two_a = move(two_a, ACROSS, "across2A")
    over_two_b = move(two_b, ACROSS, "across2B")
    have = [
        [both, low, high],
        [over, two_a, two_b],
        [over_low, over_high, over_two_a, over_two_b],
    ]
    return oth, cot_oth, have


def scattered(pieces):
    cross_low = move(pieces[1, 1], UP, "upX")
    cross_high = move(pieces[1, -1], DOWN, "downX")
    far = move(pieces[1, 2], ACROSS, "far")
    via_a = move(added(pieces[0, 2][0], far[0]), UP, "viaA")
    via_b = move(added(pieces[0, 2][1], far[1]), DOWN, "viaB")
    up_b = move(after(pieces[0, 1][1], cross_low), UP, "upB")
    down_a = move(after(pieces[0, -1][0], cross_high), DOWN, "downA")
    crossed = move(added(pieces[1, 0], cross_low, cross_high), ACROSS, "crossed")
    up_a = move(added(pieces[0, 1][0], via_a), UP, "upA")
    down_b = move(added(pieces[0, -1][1], via_b), DOWN, "downB")
    return pieces[0, 0], up_a, up_b, down_a, down_b, crossed


def later(f, own, oth, slope):
    n = len(LATER)
    out = pl.pallas_call(
        grad_kernel,
        out_shape=[shape(2, HALF, ROWS)] * n,
        in_specs=[SMEM, ANY, ANY, VMEM],
        out_specs=[ANY] * n,
        scratch_shapes=[
            pltpu.VMEM((n, 2 * ROWS, 2 * ROWS), BF),
            pltpu.VMEM((n, 2, HALF, ROWS), BF),
            pltpu.SemaphoreType.DMA((n, 2)),
            pltpu.SemaphoreType.DMA((n,)),
        ],
        compiler_params=PARAMS,
        cost_estimate=pl.CostEstimate(flops=n * HALF * 2**19, bytes_accessed=n * 2**20, transcendentals=0),
        name="grad",
    )(f, own, oth, slope)
    return dict(zip(LATER, out))


def ahead(offset, f, weight, moved, sent, first, second, kept, swapped):
    routes = [((i - offset) % 16, i) for i in range(16)]
    weight_arrived, arrived = (lax.ppermute(a, "rep", routes) for a in (weight, sent))
    cost = pl.CostEstimate(flops=2**22, bytes_accessed=8 * 2**20, transcendentals=0)
    new_first, new_second = pl.pallas_call(
        moment_kernel,
        out_shape=[shape(FF, ROWS, dtype=F32)] * 2,
        in_specs=[SMEM] + [VMEM] * 4,
        out_specs=[VMEM] * 2,
        compiler_params=PARAMS,
        cost_estimate=cost,
        name="moments",
    )(f, first, second, kept, swapped)
    mixed = pl.pallas_call(
        mix_kernel,
        out_shape=shape(FF, ROWS, dtype=F32),
        in_specs=[SMEM, VMEM, VMEM],
        out_specs=ANY,
        scratch_shapes=[pltpu.VMEM((2, HALF, ROWS), F32), pltpu.SemaphoreType.DMA((2, 2))],
        compiler_params=PARAMS,
        cost_estimate=cost,
        name="mix",
    )(f, moved, arrived)
    return mixed, new_first, new_second, 0.5 * (weight + weight_arrived)


def on_device(params, first, second, weight, tokens, cotangent, step):
    f = lax.axis_index("fsdp").astype(jnp.int32).reshape(1)
    step = step.reshape(1)
    params, first, second = (a[0].T for a in (params, first, second))
    own, cot = tokens[0], cotangent[0].T
    mine, other = pl.pallas_call(
        cast_kernel,
        out_shape=[shape(2, HALF, ROWS), shape(HALF, ROWS)],
        in_specs=[SMEM, SMEM, VMEM],
        out_specs=[VMEM, VMEM],
        compiler_params=PARAMS,
        name="cast",
    )(f, weight, params)
    cot_sent = lax.dynamic_slice(cot, ((1 - (f[0] & 1)) * HALF, 0), (HALF, ROWS))
    oth, cot_oth, have = gather(mine, other, own, cot_sent)

    def stage(k, kernel, specs, *more, outs=0, extra=()):
        n = len(STAGES[k])
        return pl.pallas_call(
            kernel,
            out_shape=[shape(HALF, 2 * ROWS, dtype=BF if outs else F32)] + [shape(2, HALF, ROWS)] * outs,
            in_specs=[SMEM, ANY, ANY] + specs + [ANY] * len(have[k]),
            out_specs=[VMEM] + [ANY] * outs,
            scratch_shapes=[
                pltpu.VMEM((max(n, outs), 2 * ROWS, 2 * ROWS), BF),
                pltpu.VMEM((n, HALF, 2 * ROWS), BF),
                pltpu.SemaphoreType.DMA((max(n, outs), 4)),
            ]
            + list(extra),
            compiler_params=PARAMS,
            cost_estimate=pl.CostEstimate(
                flops=(n + outs) * HALF * 2**19, bytes_accessed=n * 2**20, transcendentals=0
            ),
            name="gate" + str(k),
        )(f, own, oth, *more, *have[k])

    (total,) = stage(0, first_kernel, [])
    (total,) = stage(1, next_kernel, [VMEM], total)
    slope, *soon = stage(
        2, last_kernel, [VMEM, ANY, VMEM], total, cot, cot_oth, outs=len(SOON),
        extra=[
            pltpu.VMEM((HALF, 2 * ROWS), F32),
            pltpu.VMEM((HALF, ROWS), BF),
            pltpu.SemaphoreType.DMA,
            pltpu.VMEM((len(SOON), 2, HALF, ROWS), BF),
            pltpu.SemaphoreType.DMA((len(SOON),)),
        ],
    )
    pieces = dict(zip(SOON, soon))
    pieces.update(later(f, own, oth, slope))
    kept, other = pl.pallas_call(
        total_kernel,
        out_shape=[shape(HALF, ROWS, dtype=F32), shape(HALF, ROWS)],
        in_specs=[VMEM] * 6,
        out_specs=[VMEM] * 2,
        compiler_params=PARAMS,
        cost_estimate=pl.CostEstimate(flops=2**22, bytes_accessed=4 * 2**20, transcendentals=0),
        name="total",
    )(*scattered(pieces))
    swapped = move(other, CORE, "swap")
    moved, sent = pl.pallas_call(
        step_kernel,
        out_shape=[shape(2, HALF, ROWS, dtype=F32), shape(2, HALF, ROWS)],
        in_specs=[SMEM, SMEM] + [VMEM] * 5,
        out_specs=[VMEM, VMEM],
        compiler_params=PARAMS,
        cost_estimate=pl.CostEstimate(flops=2**24, bytes_accessed=10 * 2**20, transcendentals=0),
        name="step",
    )(f, step, params, first, second, kept, swapped)
    mixed, new_first, new_second, new_weight = lax.switch(
        step[0] & 3,
        [partial(ahead, 1 << bit) for bit in range(4)],
        f, weight, moved, sent, first, second, kept, swapped,
    )
    return mixed.T[None], new_first.T[None], new_second.T[None], new_weight


def solution(mesh):
    block = P("rep", "fsdp", None)
    in_specs = (block, block, block, P("rep"), block, block, P())
    out_specs = (block, block, block, P("rep"))
    return jax.shard_map(
        on_device, mesh=mesh, in_specs=in_specs, out_specs=out_specs, check_vma=False
    )
```

```python
from functools import partial

import jax
import jax.numpy as jnp
import numpy as np
from jax import lax
from jax.experimental import pallas as pl
from jax.experimental.pallas import tpu as pltpu
from jax.sharding import PartitionSpec as P

ANY = pl.BlockSpec(memory_space=pl.ANY)
VMEM = pl.BlockSpec(memory_space=pltpu.VMEM)
SMEM = pl.BlockSpec(memory_space=pltpu.SMEM)
BF = jnp.bfloat16
F32 = jnp.float32
PARAMS = pltpu.CompilerParams(vmem_limit_bytes=16 * 1024 * 1024)

D = 4096
FF = 1376
HALF = FF // 2
ROWS = 256

STAGES = (
    ([(0, 0), (0, -1), (0, 1)], (2, 2, 2)),
    ([(1, 0), (0, 2)], (1, 2)),
    ([(1, 2)], (2,)),
    ([(1, -1), (1, 1)], (1, 1)),
)
SOON = [(1, -1), (1, 1), (1, 2)]
LATER = [(0, 2), (0, 1), (0, -1), (1, 0), (0, 0)]


def route(move):
    pairs = []
    for f in range(16):
        x, y, c = move(f // 8, f // 2 % 4, f % 2)
        pairs.append((f, x % 2 * 8 + y % 4 * 2 + c % 2))
    return pairs


CORE = route(lambda x, y, c: (x, y, c + 1))
UP = route(lambda x, y, c: (x, y + 1, c))
DOWN = route(lambda x, y, c: (x, y - 1, c))
TWO = route(lambda x, y, c: (x, y + 2, c))
ACROSS = route(lambda x, y, c: (x + 1, y, c))


def move(block, way, name):
    with jax.named_scope(name):
        return lax.ppermute(block, "fsdp", way)


def after(block, *others):
    return lax.optimization_barrier((block, *others))[0]


def chip(f, piece):
    dx, dy = piece
    return ((f // 8 + dx) & 1) * 4 + ((f // 2 + dy) & 3)


def cast_kernel(f_ref, weight_ref, params_ref, other_ref, mine_ref, both_ref):
    c = f_ref[0] & 1
    weight = weight_ref[0]

    def half(c):
        rows = pl.ds(pl.multiple_of(c * HALF, 16), HALF)
        return (params_ref[rows, :] / weight).astype(BF)

    other_ref[...] = half(1 - c)
    mine = half(c)
    mine_ref[...] = mine
    both_ref[0] = mine


def token_copies(f, pieces, own_ref, oth_ref, buf, sems):
    copies = []
    for i, piece in enumerate(pieces):
        cols = pl.ds(pl.multiple_of(chip(f, piece) * 2 * ROWS, 2 * ROWS), 2 * ROWS)
        copies.append(
            (
                pltpu.make_async_copy(own_ref.at[:, cols], buf.at[i, pl.ds(0, ROWS)], sems.at[i, 0]),
                pltpu.make_async_copy(oth_ref.at[:, cols], buf.at[i, pl.ds(ROWS, ROWS)], sems.at[i, 1]),
            )
        )
    return copies


def gate_sum(
    f, pieces, own_ref, oth_ref, weights, tok, wbuf, sems, start_ref, out_ref, extra=()
):
    c = f & 1
    copies = token_copies(f, pieces, own_ref, oth_ref, tok, sems)
    for i in range(len(pieces)):
        blocks = ()
        for ab in range(2):
            cols = pl.ds(pl.multiple_of((c ^ ab) * ROWS, ROWS), ROWS)
            blocks += (pltpu.make_async_copy(weights[i][ab], wbuf.at[i, :, cols], sems.at[i, 2 + ab]),)
        copies[i] += blocks
    for group in [*copies, *extra]:
        for copy in group:
            copy.start()
    for i, group in enumerate(copies):
        for copy in group:
            copy.wait()
        term = lax.dot_general(
            wbuf[i], tok[i], (((1,), (1,)), ((), ())), preferred_element_type=F32
        )
        if i > 0:
            out_ref[...] += term
        elif start_ref is None:
            out_ref[...] = term
        else:
            out_ref[...] = start_ref[...] + term


def paired(refs, counts):
    out = []
    for count in counts:
        out.append((refs[0].at[0], refs[0].at[1]) if count == 1 else refs[:2])
        refs = refs[count:]
    return out, refs


def stage_kernel(k, f_ref, own_ref, oth_ref, *refs):
    pieces, counts = STAGES[k]
    sum_ref, refs = (refs[0], refs[1:]) if k else (None, refs)
    weights, (out_ref, tok, wbuf, sems) = paired(refs, counts)
    gate_sum(f_ref[0], pieces, own_ref, oth_ref, weights, tok, wbuf, sems, sum_ref, out_ref)


def last_kernel(f_ref, own_ref, oth_ref, sum_ref, cot_ref, cot_oth_ref, *refs):
    pieces, counts = STAGES[-1]
    weights, refs = paired(refs, counts)
    slope_ref, *outs = refs[:4]
    tok, wbuf, sems, gate, cot, cot_sem, res, out_sems = refs[4:]
    f = f_ref[0]
    c = f & 1
    rows = pl.ds(pl.multiple_of(c * HALF, 16), HALF)
    cot_copy = pltpu.make_async_copy(cot_ref.at[rows, :], cot, cot_sem)
    cot_copy.start()
    extra = token_copies(f, SOON, own_ref, oth_ref, tok, sems)[len(pieces) :]
    gate_sum(f, pieces, own_ref, oth_ref, weights, tok, wbuf, sems, sum_ref, gate, extra)
    cot_copy.wait()

    def body(i, carry):
        rows = pl.ds(pl.multiple_of(i * 16, 16), 16)
        for half, part in ((0, cot), (1, cot_oth_ref)):
            cols = slice(half * ROWS, half * ROWS + ROWS)
            g = gate[rows, cols]
            sig = 1.0 / (1.0 + jnp.exp(-g))
            slope_ref[rows, cols] = (
                part[rows, :].astype(F32) * sig * (1.0 + g * (1.0 - sig))
            ).astype(BF)
        return carry

    lax.fori_loop(0, HALF // 16, body, 0)
    for pair in extra:
        for copy in pair:
            copy.wait()
    grad_loop(c, slope_ref, tok, res, outs, out_sems, None)


def grad_loop(c, slope_ref, tok, res, outs, out_sems, arrival):
    def write(i):
        return pltpu.make_async_copy(res.at[i], outs[i], out_sems.at[i])

    def body(i, carry):
        if arrival is not None:
            arrival(i)
        both = jnp.dot(slope_ref[...], tok[i], preferred_element_type=F32).astype(BF)
        for core in range(2):
            res[i, c ^ core] = both[:, core * ROWS : core * ROWS + ROWS]
        for j in range(len(outs)):

            @pl.when(i == j)
            def _():
                write(j).start()

        return carry

    lax.fori_loop(0, len(outs), body, 0)
    for i in range(len(outs)):
        write(i).wait()


def grad_kernel(f_ref, own_ref, oth_ref, slope_ref, *refs):
    n = len(LATER)
    outs, (tok, res, sems, out_sems) = refs[:n], refs[n:]
    f = f_ref[0]
    for pair in token_copies(f, LATER, own_ref, oth_ref, tok, sems):
        for copy in pair:
            copy.start()

    def arrival(i):
        for j, src in enumerate((own_ref, oth_ref)):
            pltpu.make_async_copy(
                src.at[:, pl.ds(0, 2 * ROWS)], tok.at[i, pl.ds(j * ROWS, ROWS)], sems.at[i, j]
            ).wait()

    grad_loop(f & 1, slope_ref, tok, res, outs, out_sems, arrival)


LOG_ONE = np.log(np.float32(0.9))
LOG_TWO = np.log(np.float32(0.999))


def rows_of(c, i, t):
    half = c if i == 0 else 1 - c
    return pl.ds(pl.multiple_of(half * HALF + t * 16, 16), 16)


def total_kernel(base, up_a, up_b, down_a, down_b, crossed, kept_ref, sent_ref):
    def body(t, carry):
        at = pl.ds(pl.multiple_of(t * 16, 16), 16)
        for i, up, down in ((0, up_a, down_a), (1, up_b, down_b)):
            total = base[i, at].astype(F32) + up[at].astype(F32)
            total = total + down[at].astype(F32) + crossed[i, at].astype(F32)
            if i == 0:
                kept_ref[at] = total
            else:
                sent_ref[at] = total.astype(BF)
        return carry

    lax.fori_loop(0, HALF // 16, body, 0)


def grad_rows(kept, swapped, i, at):
    return kept[at] if i == 0 else swapped[at].astype(F32)


def step_kernel(
    f_ref, step_ref, weight_ref, params_ref, first_ref, second_ref, kept, swapped, moved_ref, sent_ref
):
    c = f_ref[0] & 1
    stepf = jnp.full((1, ROWS), step_ref[0], jnp.int32).astype(F32) + 1.0
    rate = 0.01 * jnp.minimum(1.0, stepf / 2000.0)
    corr_one = 1.0 / (1.0 - jnp.exp(stepf * LOG_ONE))
    corr_two = 1.0 / (1.0 - jnp.exp(stepf * LOG_TWO))

    def tile(t):
        at = pl.ds(pl.multiple_of(t * 16, 16), 16)
        done = []
        for i in range(2):
            rows = rows_of(c, i, t)
            grad = grad_rows(kept, swapped, i, at)
            new_first = 0.9 * first_ref[rows] + 0.1 * grad
            new_second = 0.999 * second_ref[rows] + 0.001 * grad * grad
            master = params_ref[rows]
            update = new_first * corr_one / (jnp.sqrt(new_second * corr_two) + 1e-08)
            done.append((i, t, master - rate * (update + 0.1 * master)))
        return done

    def store(done):
        for i, t, moved in done:
            at = pl.ds(pl.multiple_of(i * HALF + t * 16, 16), 16)
            moved_ref[at] = 0.5 * moved
            sent_ref[at] = moved.astype(BF)

    def body(t, carry):
        store(tile(3 * t) + tile(3 * t + 1) + tile(3 * t + 2))
        return carry

    lax.fori_loop(0, HALF // 48, body, 0)
    store(tile(HALF // 16 - 1))
    sent_ref[FF:] = jnp.full((16, ROWS), weight_ref[0], F32).astype(BF)


def moment_kernel(f_ref, first_ref, second_ref, kept, swapped, first_out, second_out):
    c = f_ref[0] & 1

    def body(t, carry):
        at = pl.ds(pl.multiple_of(t * 16, 16), 16)
        for i in range(2):
            rows = rows_of(c, i, t)
            grad = grad_rows(kept, swapped, i, at)
            first_out[rows] = 0.9 * first_ref[rows] + 0.1 * grad
            second_out[rows] = 0.999 * second_ref[rows] + 0.001 * grad * grad
        return carry

    lax.fori_loop(0, HALF // 16, body, 0)


def mix_kernel(f_ref, weight_ref, moved_ref, arrived_ref, out_ref, weight_out, buf, sems):
    c = f_ref[0] & 1
    copies = []
    for k, (lo, size) in enumerate(((0, 352), (352, 336))):
        for i in range(2):
            half = c if i == 0 else 1 - c
            rows = pl.ds(pl.multiple_of(half * HALF + lo, 16), size)
            copies.append(
                pltpu.make_async_copy(
                    buf.at[pl.ds(i * HALF + lo, size)], out_ref.at[rows], sems.at[k, i]
                )
            )

        def body(t, carry):
            for i in range(2):
                at = pl.ds(pl.multiple_of(i * HALF + lo + t * 16, 16), 16)
                buf[at] = moved_ref[at] + 0.5 * arrived_ref[at].astype(F32)
            return carry

        lax.fori_loop(0, size // 16, body, 0)
        for copy in copies[-2:]:
            copy.start()
    arrived = arrived_ref[FF:, :128].astype(F32)
    weight_out[0] = 0.5 * (weight_ref[0] + arrived[0, 0])
    for copy in copies:
        copy.wait()


def shape(*dims, dtype=BF):
    return jax.ShapeDtypeStruct(dims, dtype)


def added(*terms):
    total = terms[0].astype(F32)
    for term in terms[1:]:
        total = total + term.astype(F32)
    return total.astype(BF)


def gather(other, mine, both, own, cot_sent):
    low_a = move(mine, UP, "upA")
    b = move(other, CORE, "B")
    high_b = move(b, DOWN, "downB")
    low_b = move(b, UP, "upB")
    high_a = move(after(mine, b), DOWN, "downA")
    oth = move(after(own, b), CORE, "tokens")
    over = move(lax.dynamic_update_slice(both, b[None], (1, 0, 0)), ACROSS, "across")
    two_a = move(low_a, UP, "twoA")
    two_b = move(high_b, DOWN, "twoB")
    cot_oth = move(after(cot_sent, oth), CORE, "cotangent")
    over_late = after(over, oth, cot_oth, two_a, two_b, low_b, high_a)
    over_low = move(over_late, UP, "upX")
    over_high = move(over_late, DOWN, "downX")
    over_two_a = move(two_a, ACROSS, "across2A")
    over_two_b = move(two_b, ACROSS, "across2B")
    have = [
        [mine, b, low_a, low_b, high_a, high_b],
        [over, two_a, two_b],
        [over_two_a, over_two_b],
        [over_low, over_high],
    ]
    return oth, cot_oth, have


def scattered(pieces):
    cross_low = move(pieces[1, 1], UP, "upX")
    cross_high = move(pieces[1, -1], DOWN, "downX")
    far = move(pieces[1, 2], ACROSS, "far")
    via_a = move(added(pieces[0, 2][0], far[0]), UP, "viaA")
    via_b = move(added(pieces[0, 2][1], far[1]), DOWN, "viaB")
    up_b = move(after(pieces[0, 1][1], cross_low), UP, "upB")
    down_a = move(after(pieces[0, -1][0], cross_high), DOWN, "downA")
    crossed = move(added(pieces[1, 0], cross_low, cross_high), ACROSS, "crossed")
    up_a = move(added(pieces[0, 1][0], via_a), UP, "upA")
    down_b = move(added(pieces[0, -1][1], via_b), DOWN, "downB")
    return pieces[0, 0], up_a, up_b, down_a, down_b, crossed


def later(f, own, oth, slope):
    n = len(LATER)
    out = pl.pallas_call(
        grad_kernel,
        out_shape=[shape(2, HALF, ROWS)] * n,
        in_specs=[SMEM, ANY, ANY, VMEM],
        out_specs=[ANY] * n,
        scratch_shapes=[
            pltpu.VMEM((n, 2 * ROWS, 2 * ROWS), BF),
            pltpu.VMEM((n, 2, HALF, ROWS), BF),
            pltpu.SemaphoreType.DMA((n, 2)),
            pltpu.SemaphoreType.DMA((n,)),
        ],
        compiler_params=PARAMS,
        cost_estimate=pl.CostEstimate(flops=n * HALF * 2**19, bytes_accessed=n * 2**20, transcendentals=0),
        name="grad",
    )(f, own, oth, slope)
    return dict(zip(LATER, out))


def ahead(offset, f, sent, first, second, kept, swapped):
    arrived = lax.ppermute(sent, "rep", [((i - offset) % 16, i) for i in range(16)])
    new_first, new_second = pl.pallas_call(
        moment_kernel,
        out_shape=[shape(FF, ROWS, dtype=F32)] * 2,
        in_specs=[SMEM] + [VMEM] * 4,
        out_specs=[VMEM] * 2,
        compiler_params=PARAMS,
        cost_estimate=pl.CostEstimate(flops=2**22, bytes_accessed=8 * 2**20, transcendentals=0),
        name="moments",
    )(f, first, second, kept, swapped)
    return arrived, new_first, new_second


def on_device(params, first, second, weight, tokens, cotangent, step):
    f = lax.axis_index("fsdp").astype(jnp.int32).reshape(1)
    step = step.reshape(1)
    params, first, second = (a[0].T for a in (params, first, second))
    own, cot = tokens[0], cotangent[0].T
    other, mine, both = pl.pallas_call(
        cast_kernel,
        out_shape=[shape(HALF, ROWS), shape(HALF, ROWS), shape(2, HALF, ROWS)],
        in_specs=[SMEM, SMEM, VMEM],
        out_specs=[VMEM] * 3,
        compiler_params=PARAMS,
        name="cast",
    )(f, weight, params)
    cot_sent = lax.dynamic_slice(cot, ((1 - (f[0] & 1)) * HALF, 0), (HALF, ROWS))
    oth, cot_oth, have = gather(other, mine, both, own, cot_sent)

    def stage(k, kernel, specs, *more, outs=0, extra=()):
        n = len(STAGES[k][0])
        return pl.pallas_call(
            kernel,
            out_shape=[shape(HALF, 2 * ROWS, dtype=BF if outs else F32)] + [shape(2, HALF, ROWS)] * outs,
            in_specs=[SMEM, ANY, ANY] + specs + [ANY] * len(have[k]),
            out_specs=[VMEM] + [ANY] * outs,
            scratch_shapes=[
                pltpu.VMEM((max(n, outs), 2 * ROWS, 2 * ROWS), BF),
                pltpu.VMEM((n, HALF, 2 * ROWS), BF),
                pltpu.SemaphoreType.DMA((max(n, outs), 4)),
            ]
            + list(extra),
            compiler_params=PARAMS,
            cost_estimate=pl.CostEstimate(
                flops=(n + outs) * HALF * 2**19, bytes_accessed=n * 2**20, transcendentals=0
            ),
            name="gate" + str(k),
        )(f, own, oth, *more, *have[k])

    (total,) = stage(0, partial(stage_kernel, 0), [])
    (total,) = stage(1, partial(stage_kernel, 1), [VMEM], total)
    (total,) = stage(2, partial(stage_kernel, 2), [VMEM], total)
    slope, *soon = stage(
        3, last_kernel, [VMEM, ANY, VMEM], total, cot, cot_oth, outs=len(SOON),
        extra=[
            pltpu.VMEM((HALF, 2 * ROWS), F32),
            pltpu.VMEM((HALF, ROWS), BF),
            pltpu.SemaphoreType.DMA,
            pltpu.VMEM((len(SOON), 2, HALF, ROWS), BF),
            pltpu.SemaphoreType.DMA((len(SOON),)),
        ],
    )
    pieces = dict(zip(SOON, soon))
    pieces.update(later(f, own, oth, slope))
    kept, other = pl.pallas_call(
        total_kernel,
        out_shape=[shape(HALF, ROWS, dtype=F32), shape(HALF, ROWS)],
        in_specs=[VMEM] * 6,
        out_specs=[VMEM] * 2,
        compiler_params=PARAMS,
        cost_estimate=pl.CostEstimate(flops=2**22, bytes_accessed=4 * 2**20, transcendentals=0),
        name="total",
    )(*scattered(pieces))
    swapped = move(other, CORE, "swap")
    moved, sent = pl.pallas_call(
        step_kernel,
        out_shape=[shape(FF, ROWS, dtype=F32), shape(FF + 16, ROWS)],
        in_specs=[SMEM, SMEM, SMEM] + [VMEM] * 5,
        out_specs=[VMEM, VMEM],
        compiler_params=PARAMS,
        cost_estimate=pl.CostEstimate(flops=2**24, bytes_accessed=10 * 2**20, transcendentals=0),
        name="step",
    )(f, step, weight, params, first, second, kept, swapped)
    arrived, new_first, new_second = lax.switch(
        step[0] & 3,
        [partial(ahead, 1 << bit) for bit in range(4)],
        f, sent, first, second, kept, swapped,
    )
    mixed, new_weight = pl.pallas_call(
        mix_kernel,
        out_shape=[shape(FF, ROWS, dtype=F32), shape(1, dtype=F32)],
        in_specs=[SMEM, SMEM, VMEM, VMEM],
        out_specs=[ANY, SMEM],
        scratch_shapes=[pltpu.VMEM((FF, ROWS), F32), pltpu.SemaphoreType.DMA((2, 2))],
        compiler_params=PARAMS,
        name="mix",
    )(f, weight, moved, arrived)
    return mixed.T[None], new_first.T[None], new_second.T[None], new_weight


def solution(mesh):
    block = P("rep", "fsdp", None)
    in_specs = (block, block, block, P("rep"), block, block, P())
    out_specs = (block, block, block, P("rep"))
    return jax.shard_map(
        on_device, mesh=mesh, in_specs=in_specs, out_specs=out_specs, check_vma=False
    )
```

```python
from functools import partial

import jax
import jax.numpy as jnp
import numpy as np
from jax import lax
from jax.experimental import pallas as pl
from jax.experimental.pallas import tpu as pltpu
from jax.sharding import PartitionSpec as P

ANY = pl.BlockSpec(memory_space=pl.ANY)
VMEM = pl.BlockSpec(memory_space=pltpu.VMEM)
SMEM = pl.BlockSpec(memory_space=pltpu.SMEM)
BF = jnp.bfloat16
F32 = jnp.float32
PARAMS = pltpu.CompilerParams(vmem_limit_bytes=18 * 1024 * 1024)

D = 4096
FF = 1376
HALF = FF // 2
ROWS = 256

STAGES = (
    ([(0, 0), (0, -1), (0, 1)], (2, 2, 2)),
    ([(1, 0), (0, 2)], (1, 2)),
    ([(1, 2)], (2,)),
    ([(1, -1), (1, 1)], (1, 1)),
)
SOON = [(1, -1), (1, 1), (1, 2)]
LATER = [(0, 2), (0, 1), (0, -1), (1, 0), (0, 0)]


def route(move):
    pairs = []
    for f in range(16):
        x, y, c = move(f // 8, f // 2 % 4, f % 2)
        pairs.append((f, x % 2 * 8 + y % 4 * 2 + c % 2))
    return pairs


CORE = route(lambda x, y, c: (x, y, c + 1))
UP = route(lambda x, y, c: (x, y + 1, c))
DOWN = route(lambda x, y, c: (x, y - 1, c))
TWO = route(lambda x, y, c: (x, y + 2, c))
ACROSS = route(lambda x, y, c: (x + 1, y, c))


def move(block, way, name):
    with jax.named_scope(name):
        return lax.ppermute(block, "fsdp", way)


def after(block, *others):
    return lax.optimization_barrier((block, *others))[0]


def chip(f, piece):
    dx, dy = piece
    return ((f // 8 + dx) & 1) * 4 + ((f // 2 + dy) & 3)


def cast_kernel(f_ref, weight_ref, params_ref, other_ref, mine_ref, both_ref):
    c = f_ref[0] & 1
    weight = weight_ref[0]

    def half(c):
        rows = pl.ds(pl.multiple_of(c * HALF, 16), HALF)
        return (params_ref[rows, :] / weight).astype(BF)

    other_ref[...] = half(1 - c)
    mine = half(c)
    mine_ref[...] = mine
    both_ref[0] = mine


def token_copies(f, pieces, own_ref, oth_ref, buf, sems):
    copies = []
    for i, piece in enumerate(pieces):
        cols = pl.ds(pl.multiple_of(chip(f, piece) * 2 * ROWS, 2 * ROWS), 2 * ROWS)
        copies.append(
            (
                pltpu.make_async_copy(own_ref.at[:, cols], buf.at[i, pl.ds(0, ROWS)], sems.at[i, 0]),
                pltpu.make_async_copy(oth_ref.at[:, cols], buf.at[i, pl.ds(ROWS, ROWS)], sems.at[i, 1]),
            )
        )
    return copies


def gate_sum(
    f, pieces, own_ref, oth_ref, weights, tok, wbuf, sems, start_ref, out_ref, extra=()
):
    c = f & 1
    copies = token_copies(f, pieces, own_ref, oth_ref, tok, sems)
    for i in range(len(pieces)):
        blocks = ()
        for ab in range(2):
            cols = pl.ds(pl.multiple_of((c ^ ab) * ROWS, ROWS), ROWS)
            blocks += (pltpu.make_async_copy(weights[i][ab], wbuf.at[i, :, cols], sems.at[i, 2 + ab]),)
        copies[i] += blocks
    for group in [*copies, *extra]:
        for copy in group:
            copy.start()
    for i, group in enumerate(copies):
        for copy in group:
            copy.wait()
        term = lax.dot_general(
            wbuf[i], tok[i], (((1,), (1,)), ((), ())), preferred_element_type=F32
        )
        if i > 0:
            out_ref[...] += term
        elif start_ref is None:
            out_ref[...] = term
        else:
            out_ref[...] = start_ref[...] + term


def paired(refs, counts):
    out = []
    for count in counts:
        out.append((refs[0].at[0], refs[0].at[1]) if count == 1 else refs[:2])
        refs = refs[count:]
    return out, refs


def stage_kernel(k, f_ref, own_ref, oth_ref, *refs):
    pieces, counts = STAGES[k]
    sum_ref, refs = (refs[0], refs[1:]) if k else (None, refs)
    weights, (out_ref, tok, wbuf, sems) = paired(refs, counts)
    gate_sum(f_ref[0], pieces, own_ref, oth_ref, weights, tok, wbuf, sems, sum_ref, out_ref)


def last_kernel(f_ref, own_ref, oth_ref, sum_ref, cot_ref, cot_oth_ref, *refs):
    pieces, counts = STAGES[-1]
    weights, refs = paired(refs, counts)
    slope_ref, *outs = refs[:4]
    tok, wbuf, sems, gate, cot, cot_sem, res, out_sems = refs[4:]
    f = f_ref[0]
    c = f & 1
    rows = pl.ds(pl.multiple_of(c * HALF, 16), HALF)
    cot_copy = pltpu.make_async_copy(cot_ref.at[rows, :], cot, cot_sem)
    cot_copy.start()
    extra = token_copies(f, SOON, own_ref, oth_ref, tok, sems)[len(pieces) :]
    gate_sum(f, pieces, own_ref, oth_ref, weights, tok, wbuf, sems, sum_ref, gate, extra)
    cot_copy.wait()

    def slopes(start, size):
        rows = pl.ds(pl.multiple_of(start, 16), size)
        done = []
        for half, part in ((0, cot), (1, cot_oth_ref)):
            cols = slice(half * ROWS, half * ROWS + ROWS)
            g = gate[rows, cols]
            sig = 1.0 / (1.0 + jnp.exp(-g))
            done.append((cols, part[rows, :].astype(F32) * sig * (1.0 + g * (1.0 - sig))))
        for cols, slope in done:
            slope_ref[rows, cols] = slope.astype(BF)

    def body(i, carry):
        slopes(i * 48, 48)
        return carry

    lax.fori_loop(0, HALF // 48, body, 0)
    slopes(HALF - 16, 16)
    for pair in extra:
        for copy in pair:
            copy.wait()
    grad_loop(c, slope_ref, tok, res, outs, out_sems, None)


def grad_loop(c, slope_ref, tok, res, outs, out_sems, arrival):
    def write(i):
        return pltpu.make_async_copy(res.at[i], outs[i], out_sems.at[i])

    def body(i, carry):
        if arrival is not None:
            arrival(i)
        both = jnp.dot(slope_ref[...], tok[i], preferred_element_type=F32).astype(BF)
        for core in range(2):
            res[i, c ^ core] = both[:, core * ROWS : core * ROWS + ROWS]
        for j in range(len(outs)):

            @pl.when(i == j)
            def _():
                write(j).start()

        return carry

    lax.fori_loop(0, len(outs), body, 0)
    for i in range(len(outs)):
        write(i).wait()


def grad_kernel(f_ref, own_ref, oth_ref, slope_ref, *refs):
    n = len(LATER)
    outs, (tok, res, sems, out_sems) = refs[:n], refs[n:]
    f = f_ref[0]
    for pair in token_copies(f, LATER, own_ref, oth_ref, tok, sems):
        for copy in pair:
            copy.start()

    def arrival(i):
        for j, src in enumerate((own_ref, oth_ref)):
            pltpu.make_async_copy(
                src.at[:, pl.ds(0, 2 * ROWS)], tok.at[i, pl.ds(j * ROWS, ROWS)], sems.at[i, j]
            ).wait()

    grad_loop(f & 1, slope_ref, tok, res, outs, out_sems, arrival)


LOG_ONE = np.log(np.float32(0.9))
LOG_TWO = np.log(np.float32(0.999))


def rows_of(c, i, t):
    half = c if i == 0 else 1 - c
    return pl.ds(pl.multiple_of(half * HALF + t * 16, 16), 16)


def total_kernel(base, up_a, up_b, down_a, down_b, crossed, kept_ref, sent_ref):
    def body(t, carry):
        at = pl.ds(pl.multiple_of(t * 16, 16), 16)
        for i, up, down in ((0, up_a, down_a), (1, up_b, down_b)):
            total = base[i, at].astype(F32) + up[at].astype(F32)
            total = total + down[at].astype(F32) + crossed[i, at].astype(F32)
            if i == 0:
                kept_ref[at] = total
            else:
                sent_ref[at] = total.astype(BF)
        return carry

    lax.fori_loop(0, HALF // 16, body, 0)


def grad_rows(kept, swapped, i, at):
    return kept[at] if i == 0 else swapped[at].astype(F32)


def step_kernel(
    f_ref, step_ref, weight_ref, params_ref, first_ref, second_ref, kept, swapped,
    sent_ref, first_out, second_out, first_buf, second_buf, sems,
):
    c = f_ref[0] & 1
    stepf = jnp.full((1, ROWS), step_ref[0], jnp.int32).astype(F32) + 1.0
    rate = 0.01 * jnp.minimum(1.0, stepf / 2000.0)
    corr_one = 1.0 / (1.0 - jnp.exp(stepf * LOG_ONE))
    corr_two = 1.0 / (1.0 - jnp.exp(stepf * LOG_TWO))

    def tile(t):
        at = pl.ds(pl.multiple_of(t * 16, 16), 16)
        done = []
        for i in range(2):
            rows = rows_of(c, i, t)
            grad = grad_rows(kept, swapped, i, at)
            new_first = 0.9 * first_ref[rows] + 0.1 * grad
            new_second = 0.999 * second_ref[rows] + 0.001 * grad * grad
            master = params_ref[rows]
            update = new_first * corr_one / (jnp.sqrt(new_second * corr_two) + 1e-08)
            done.append((i, t, master - rate * (update + 0.1 * master), new_first, new_second))
        return done

    def store(done):
        for i, t, moved, new_first, new_second in done:
            at = pl.ds(pl.multiple_of(i * HALF + t * 16, 16), 16)
            sent_ref[at] = moved.astype(BF)
            first_buf[at] = new_first
            second_buf[at] = new_second

    def body(t, carry):
        store(tile(3 * t) + tile(3 * t + 1) + tile(3 * t + 2))
        return carry

    copies = []
    for k, (lo, size) in enumerate(((0, 336), (336, 336))):
        lax.fori_loop(lo // 48, (lo + size) // 48, body, 0)
        if k == 1:
            store(tile(HALF // 16 - 1))
            size += 16
        for i in range(2):
            half = c if i == 0 else 1 - c
            rows = pl.ds(pl.multiple_of(half * HALF + lo, 16), size)
            at = pl.ds(i * HALF + lo, size)
            for j, (buf, out) in enumerate(((first_buf, first_out), (second_buf, second_out))):
                copies.append(pltpu.make_async_copy(buf.at[at], out.at[rows], sems.at[k, i, j]))
                copies[-1].start()
    sent_ref[FF:] = jnp.full((16, ROWS), weight_ref[0], F32).astype(BF)
    for copy in copies:
        copy.wait()


def mix_kernel(f_ref, weight_ref, sent_ref, arrived_ref, out_ref, weight_out, buf, sems):
    c = f_ref[0] & 1
    stores = []
    for k, (i, lo, size, tile) in enumerate(
        (i, *part) for part in ((0, 352, 176), (352, 336, 112)) for i in range(2)
    ):

        def body(t, carry):
            at = pl.ds(pl.multiple_of(i * HALF + lo + t * tile, 16), tile)
            buf[at] = 0.5 * (sent_ref[at].astype(F32) + arrived_ref[at].astype(F32))
            return carry

        lax.fori_loop(0, size // tile, body, 0)
        half = c if i == 0 else 1 - c
        rows = pl.ds(pl.multiple_of(half * HALF + lo, 16), size)
        stores.append(
            pltpu.make_async_copy(buf.at[pl.ds(i * HALF + lo, size)], out_ref.at[rows], sems.at[k])
        )
        stores[-1].start()
    arrived = arrived_ref[FF:, :128].astype(F32)
    weight_out[0] = 0.5 * (weight_ref[0] + arrived[0, 0])
    for copy in stores:
        copy.wait()


def shape(*dims, dtype=BF):
    return jax.ShapeDtypeStruct(dims, dtype)


def added(*terms):
    total = terms[0].astype(F32)
    for term in terms[1:]:
        total = total + term.astype(F32)
    return total.astype(BF)


def gather(other, mine, both, own, cot_sent):
    low_a = move(mine, UP, "upA")
    b = move(other, CORE, "B")
    high_b = move(b, DOWN, "downB")
    low_b = move(b, UP, "upB")
    high_a = move(after(mine, b), DOWN, "downA")
    oth = move(after(own, b), CORE, "tokens")
    over = move(lax.dynamic_update_slice(both, b[None], (1, 0, 0)), ACROSS, "across")
    two_a = move(low_a, UP, "twoA")
    two_b = move(high_b, DOWN, "twoB")
    cot_oth = move(after(cot_sent, oth), CORE, "cotangent")
    over_late = after(over, oth, cot_oth, two_a, two_b, low_b, high_a)
    over_low = move(over_late, UP, "upX")
    over_high = move(over_late, DOWN, "downX")
    over_two_a = move(two_a, ACROSS, "across2A")
    over_two_b = move(two_b, ACROSS, "across2B")
    have = [
        [mine, b, low_a, low_b, high_a, high_b],
        [over, two_a, two_b],
        [over_two_a, over_two_b],
        [over_low, over_high],
    ]
    return oth, cot_oth, have


def scattered(pieces):
    cross_low = move(pieces[1, 1], UP, "upX")
    cross_high = move(pieces[1, -1], DOWN, "downX")
    far = move(pieces[1, 2], ACROSS, "far")
    via_a = move(added(pieces[0, 2][0], far[0]), UP, "viaA")
    via_b = move(added(pieces[0, 2][1], far[1]), DOWN, "viaB")
    up_b = move(after(pieces[0, 1][1], cross_low), UP, "upB")
    down_a = move(after(pieces[0, -1][0], cross_high), DOWN, "downA")
    crossed = move(added(pieces[1, 0], cross_low, cross_high), ACROSS, "crossed")
    up_a = move(added(pieces[0, 1][0], via_a), UP, "upA")
    down_b = move(added(pieces[0, -1][1], via_b), DOWN, "downB")
    return pieces[0, 0], up_a, up_b, down_a, down_b, crossed


def later(f, own, oth, slope):
    n = len(LATER)
    out = pl.pallas_call(
        grad_kernel,
        out_shape=[shape(2, HALF, ROWS)] * n,
        in_specs=[SMEM, ANY, ANY, VMEM],
        out_specs=[ANY] * n,
        scratch_shapes=[
            pltpu.VMEM((n, 2 * ROWS, 2 * ROWS), BF),
            pltpu.VMEM((n, 2, HALF, ROWS), BF),
            pltpu.SemaphoreType.DMA((n, 2)),
            pltpu.SemaphoreType.DMA((n,)),
        ],
        compiler_params=PARAMS,
        cost_estimate=pl.CostEstimate(flops=n * HALF * 2**19, bytes_accessed=n * 2**20, transcendentals=0),
        name="grad",
    )(f, own, oth, slope)
    return dict(zip(LATER, out))


def ahead(offset, sent):
    return lax.ppermute(sent, "rep", [((i - offset) % 16, i) for i in range(16)])


def on_device(params, first, second, weight, tokens, cotangent, step):
    f = lax.axis_index("fsdp").astype(jnp.int32).reshape(1)
    step = step.reshape(1)
    params, first, second = (a[0].T for a in (params, first, second))
    own, cot = tokens[0], cotangent[0].T
    other, mine, both = pl.pallas_call(
        cast_kernel,
        out_shape=[shape(HALF, ROWS), shape(HALF, ROWS), shape(2, HALF, ROWS)],
        in_specs=[SMEM, SMEM, VMEM],
        out_specs=[VMEM] * 3,
        compiler_params=PARAMS,
        name="cast",
    )(f, weight, params)
    cot_sent = lax.dynamic_slice(cot, ((1 - (f[0] & 1)) * HALF, 0), (HALF, ROWS))
    oth, cot_oth, have = gather(other, mine, both, own, cot_sent)

    def stage(k, kernel, specs, *more, outs=0, extra=()):
        n = len(STAGES[k][0])
        return pl.pallas_call(
            kernel,
            out_shape=[shape(HALF, 2 * ROWS, dtype=BF if outs else F32)] + [shape(2, HALF, ROWS)] * outs,
            in_specs=[SMEM, ANY, ANY] + specs + [ANY] * len(have[k]),
            out_specs=[VMEM] + [ANY] * outs,
            scratch_shapes=[
                pltpu.VMEM((max(n, outs), 2 * ROWS, 2 * ROWS), BF),
                pltpu.VMEM((n, HALF, 2 * ROWS), BF),
                pltpu.SemaphoreType.DMA((max(n, outs), 4)),
            ]
            + list(extra),
            compiler_params=PARAMS,
            cost_estimate=pl.CostEstimate(
                flops=(n + outs) * HALF * 2**19, bytes_accessed=n * 2**20, transcendentals=0
            ),
            name="gate" + str(k),
        )(f, own, oth, *more, *have[k])

    (total,) = stage(0, partial(stage_kernel, 0), [])
    (total,) = stage(1, partial(stage_kernel, 1), [VMEM], total)
    (total,) = stage(2, partial(stage_kernel, 2), [VMEM], total)
    slope, *soon = stage(
        3, last_kernel, [VMEM, ANY, VMEM], total, cot, cot_oth, outs=len(SOON),
        extra=[
            pltpu.VMEM((HALF, 2 * ROWS), F32),
            pltpu.VMEM((HALF, ROWS), BF),
            pltpu.SemaphoreType.DMA,
            pltpu.VMEM((len(SOON), 2, HALF, ROWS), BF),
            pltpu.SemaphoreType.DMA((len(SOON),)),
        ],
    )
    pieces = dict(zip(SOON, soon))
    pieces.update(later(f, own, oth, slope))
    kept, other = pl.pallas_call(
        total_kernel,
        out_shape=[shape(HALF, ROWS, dtype=F32), shape(HALF, ROWS)],
        in_specs=[VMEM] * 6,
        out_specs=[VMEM] * 2,
        compiler_params=PARAMS,
        cost_estimate=pl.CostEstimate(flops=2**22, bytes_accessed=4 * 2**20, transcendentals=0),
        name="total",
    )(*scattered(pieces))
    swapped = move(other, CORE, "swap")
    sent, new_first, new_second = pl.pallas_call(
        step_kernel,
        out_shape=[shape(FF + 16, ROWS)] + [shape(FF, ROWS, dtype=F32)] * 2,
        in_specs=[SMEM, SMEM, SMEM] + [VMEM] * 5,
        out_specs=[VMEM, ANY, ANY],
        scratch_shapes=[pltpu.VMEM((FF, ROWS), F32)] * 2 + [pltpu.SemaphoreType.DMA((2, 2, 2))],
        compiler_params=PARAMS,
        cost_estimate=pl.CostEstimate(flops=2**24, bytes_accessed=10 * 2**20, transcendentals=0),
        name="step",
    )(f, step, weight, params, first, second, kept, swapped)
    arrived = lax.switch(step[0] & 3, [partial(ahead, 1 << bit) for bit in range(4)], sent)
    mixed, new_weight = pl.pallas_call(
        mix_kernel,
        out_shape=[shape(FF, ROWS, dtype=F32), shape(1, dtype=F32)],
        in_specs=[SMEM, SMEM, VMEM, VMEM],
        out_specs=[ANY, SMEM],
        scratch_shapes=[pltpu.VMEM((FF, ROWS), F32), pltpu.SemaphoreType.DMA((4,))],
        compiler_params=PARAMS,
        name="mix",
    )(f, weight, sent, arrived)
    return mixed.T[None], new_first.T[None], new_second.T[None], new_weight


def solution(mesh):
    block = P("rep", "fsdp", None)
    in_specs = (block, block, block, P("rep"), block, block, P())
    out_specs = (block, block, block, P("rep"))
    return jax.shard_map(
        on_device, mesh=mesh, in_specs=in_specs, out_specs=out_specs, check_vma=False
    )
```

```python
from functools import partial

import jax
import jax.numpy as jnp
import numpy as np
from jax import lax
from jax.experimental import pallas as pl
from jax.experimental.pallas import tpu as pltpu
from jax.sharding import PartitionSpec as P

ANY = pl.BlockSpec(memory_space=pl.ANY)
VMEM = pl.BlockSpec(memory_space=pltpu.VMEM)
SMEM = pl.BlockSpec(memory_space=pltpu.SMEM)
BF = jnp.bfloat16
F32 = jnp.float32
PARAMS = pltpu.CompilerParams(vmem_limit_bytes=18 * 1024 * 1024)

D = 4096
FF = 1376
HALF = FF // 2
ROWS = 256

STAGES = (
    ([(0, 0), (0, -1), (0, 1)], (2, 2, 2)),
    ([(1, 0), (0, 2)], (1, 2)),
    ([(1, -1), (1, 1), (1, 2)], (1, 1, 2)),
)
SOON = [(1, -1), (1, 1), (1, 2)]
LATER = [(0, 2), (0, 1), (0, -1), (1, 0), (0, 0)]


def route(move):
    pairs = []
    for f in range(16):
        x, y, c = move(f // 8, f // 2 % 4, f % 2)
        pairs.append((f, x % 2 * 8 + y % 4 * 2 + c % 2))
    return pairs


CORE = route(lambda x, y, c: (x, y, c + 1))
UP = route(lambda x, y, c: (x, y + 1, c))
DOWN = route(lambda x, y, c: (x, y - 1, c))
TWO = route(lambda x, y, c: (x, y + 2, c))
ACROSS = route(lambda x, y, c: (x + 1, y, c))


def move(block, way, name):
    with jax.named_scope(name):
        return lax.ppermute(block, "fsdp", way)


def after(block, *others):
    return lax.optimization_barrier((block, *others))[0]


def chip(f, piece):
    dx, dy = piece
    return ((f // 8 + dx) & 1) * 4 + ((f // 2 + dy) & 3)


def cast_kernel(f_ref, weight_ref, params_ref, other_ref, mine_ref, both_ref):
    c = f_ref[0] & 1
    weight = weight_ref[0]

    def half(c):
        rows = pl.ds(pl.multiple_of(c * HALF, 16), HALF)
        return (params_ref[rows, :] / weight).astype(BF)

    other_ref[...] = half(1 - c)
    mine = half(c)
    mine_ref[...] = mine
    both_ref[0] = mine


def token_copies(f, pieces, own_ref, oth_ref, buf, sems):
    copies = []
    for i, piece in enumerate(pieces):
        cols = pl.ds(pl.multiple_of(chip(f, piece) * 2 * ROWS, 2 * ROWS), 2 * ROWS)
        copies.append(
            (
                pltpu.make_async_copy(own_ref.at[:, cols], buf.at[i, pl.ds(0, ROWS)], sems.at[i, 0]),
                pltpu.make_async_copy(oth_ref.at[:, cols], buf.at[i, pl.ds(ROWS, ROWS)], sems.at[i, 1]),
            )
        )
    return copies


def gate_sum(
    f, pieces, own_ref, oth_ref, weights, tok, wbuf, sems, start_ref, out_ref, extra=()
):
    c = f & 1
    copies = token_copies(f, pieces, own_ref, oth_ref, tok, sems)
    for i in range(len(pieces)):
        blocks = ()
        for ab in range(2):
            cols = pl.ds(pl.multiple_of((c ^ ab) * ROWS, ROWS), ROWS)
            blocks += (pltpu.make_async_copy(weights[i][ab], wbuf.at[i, :, cols], sems.at[i, 2 + ab]),)
        copies[i] += blocks
    for group in [*copies, *extra]:
        for copy in group:
            copy.start()
    for i, group in enumerate(copies):
        for copy in group:
            copy.wait()
        term = lax.dot_general(
            wbuf[i], tok[i], (((1,), (1,)), ((), ())), preferred_element_type=F32
        )
        if i > 0:
            out_ref[...] += term
        elif start_ref is None:
            out_ref[...] = term
        else:
            out_ref[...] = start_ref[...] + term


def paired(refs, counts):
    out = []
    for count in counts:
        out.append((refs[0].at[0], refs[0].at[1]) if count == 1 else refs[:2])
        refs = refs[count:]
    return out, refs


def stage_kernel(k, f_ref, own_ref, oth_ref, *refs):
    pieces, counts = STAGES[k]
    sum_ref, refs = (refs[0], refs[1:]) if k else (None, refs)
    weights, (out_ref, tok, wbuf, sems) = paired(refs, counts)
    gate_sum(f_ref[0], pieces, own_ref, oth_ref, weights, tok, wbuf, sems, sum_ref, out_ref)


def last_kernel(f_ref, own_ref, oth_ref, sum_ref, cot_ref, cot_oth_ref, *refs):
    pieces, counts = STAGES[-1]
    weights, refs = paired(refs, counts)
    slope_ref, *outs = refs[:4]
    tok, wbuf, sems, gate, cot, cot_sem, res, out_sems = refs[4:]
    f = f_ref[0]
    c = f & 1
    rows = pl.ds(pl.multiple_of(c * HALF, 16), HALF)
    cot_copy = pltpu.make_async_copy(cot_ref.at[rows, :], cot, cot_sem)
    cot_copy.start()
    extra = token_copies(f, SOON, own_ref, oth_ref, tok, sems)[len(pieces) :]
    gate_sum(f, pieces, own_ref, oth_ref, weights, tok, wbuf, sems, sum_ref, gate, extra)
    cot_copy.wait()

    def slopes(start, size):
        rows = pl.ds(pl.multiple_of(start, 16), size)
        done = []
        for half, part in ((0, cot), (1, cot_oth_ref)):
            cols = slice(half * ROWS, half * ROWS + ROWS)
            g = gate[rows, cols]
            sig = 1.0 / (1.0 + jnp.exp(-g))
            done.append((cols, part[rows, :].astype(F32) * sig * (1.0 + g * (1.0 - sig))))
        for cols, slope in done:
            slope_ref[rows, cols] = slope.astype(BF)

    def body(i, carry):
        slopes(i * 48, 48)
        return carry

    lax.fori_loop(0, HALF // 48, body, 0)
    slopes(HALF - 16, 16)
    for pair in extra:
        for copy in pair:
            copy.wait()
    grad_loop(c, slope_ref, tok, res, outs, out_sems, None)


def grad_loop(c, slope_ref, tok, res, outs, out_sems, arrival):
    def write(i):
        return pltpu.make_async_copy(res.at[i], outs[i], out_sems.at[i])

    def body(i, carry):
        if arrival is not None:
            arrival(i)
        both = jnp.dot(slope_ref[...], tok[i], preferred_element_type=F32).astype(BF)
        for core in range(2):
            res[i, c ^ core] = both[:, core * ROWS : core * ROWS + ROWS]
        for j in range(len(outs)):

            @pl.when(i == j)
            def _():
                write(j).start()

        return carry

    lax.fori_loop(0, len(outs), body, 0)
    for i in range(len(outs)):
        write(i).wait()


def grad_kernel(f_ref, own_ref, oth_ref, slope_ref, *refs):
    n = len(LATER)
    outs, (tok, res, sems, out_sems) = refs[:n], refs[n:]
    f = f_ref[0]
    for pair in token_copies(f, LATER, own_ref, oth_ref, tok, sems):
        for copy in pair:
            copy.start()

    def arrival(i):
        for j, src in enumerate((own_ref, oth_ref)):
            pltpu.make_async_copy(
                src.at[:, pl.ds(0, 2 * ROWS)], tok.at[i, pl.ds(j * ROWS, ROWS)], sems.at[i, j]
            ).wait()

    grad_loop(f & 1, slope_ref, tok, res, outs, out_sems, arrival)


LOG_ONE = np.log(np.float32(0.9))
LOG_TWO = np.log(np.float32(0.999))


def rows_of(c, i, t):
    half = c if i == 0 else 1 - c
    return pl.ds(pl.multiple_of(half * HALF + t * 16, 16), 16)


def total_kernel(base, up_a, up_b, down_a, down_b, crossed, kept_ref, sent_ref):
    def body(t, carry):
        at = pl.ds(pl.multiple_of(t * 16, 16), 16)
        for i, up, down in ((0, up_a, down_a), (1, up_b, down_b)):
            total = base[i, at].astype(F32) + up[at].astype(F32)
            total = total + down[at].astype(F32) + crossed[i, at].astype(F32)
            if i == 0:
                kept_ref[at] = total
            else:
                sent_ref[at] = total.astype(BF)
        return carry

    lax.fori_loop(0, HALF // 16, body, 0)


def grad_rows(kept, swapped, i, at):
    return kept[at] if i == 0 else swapped[at].astype(F32)


def step_kernel(
    f_ref, step_ref, weight_ref, params_ref, first_ref, second_ref, kept, swapped,
    sent_ref, first_out, second_out, first_buf, second_buf, sems,
):
    c = f_ref[0] & 1
    stepf = jnp.full((1, ROWS), step_ref[0], jnp.int32).astype(F32) + 1.0
    rate = 0.01 * jnp.minimum(1.0, stepf / 2000.0)
    corr_one = 1.0 / (1.0 - jnp.exp(stepf * LOG_ONE))
    corr_two = 1.0 / (1.0 - jnp.exp(stepf * LOG_TWO))

    def tile(t):
        at = pl.ds(pl.multiple_of(t * 16, 16), 16)
        done = []
        for i in range(2):
            rows = rows_of(c, i, t)
            grad = grad_rows(kept, swapped, i, at)
            new_first = 0.9 * first_ref[rows] + 0.1 * grad
            new_second = 0.999 * second_ref[rows] + 0.001 * grad * grad
            master = params_ref[rows]
            update = new_first * corr_one / (jnp.sqrt(new_second * corr_two) + 1e-08)
            done.append((i, t, master - rate * (update + 0.1 * master), new_first, new_second))
        return done

    def store(done):
        for i, t, moved, new_first, new_second in done:
            at = pl.ds(pl.multiple_of(i * HALF + t * 16, 16), 16)
            sent_ref[at] = moved.astype(BF)
            first_buf[at] = new_first
            second_buf[at] = new_second

    def body(t, carry):
        store(tile(3 * t) + tile(3 * t + 1) + tile(3 * t + 2))
        return carry

    copies = []
    for k, (lo, size) in enumerate(((0, 336), (336, 336))):
        lax.fori_loop(lo // 48, (lo + size) // 48, body, 0)
        if k == 1:
            store(tile(HALF // 16 - 1))
            size += 16
        for i in range(2):
            half = c if i == 0 else 1 - c
            rows = pl.ds(pl.multiple_of(half * HALF + lo, 16), size)
            at = pl.ds(i * HALF + lo, size)
            for j, (buf, out) in enumerate(((first_buf, first_out), (second_buf, second_out))):
                copies.append(pltpu.make_async_copy(buf.at[at], out.at[rows], sems.at[k, i, j]))
                copies[-1].start()
    sent_ref[FF:] = jnp.full((16, ROWS), weight_ref[0], F32).astype(BF)
    for copy in copies:
        copy.wait()


def mix_kernel(f_ref, weight_ref, sent_ref, arrived_ref, out_ref, weight_out, buf, sems):
    c = f_ref[0] & 1
    stores = []
    for k, (i, lo, size, tile) in enumerate(
        (i, *part) for part in ((0, 352, 176), (352, 336, 112)) for i in range(2)
    ):

        def body(t, carry):
            at = pl.ds(pl.multiple_of(i * HALF + lo + t * tile, 16), tile)
            buf[at] = 0.5 * (sent_ref[at].astype(F32) + arrived_ref[at].astype(F32))
            return carry

        lax.fori_loop(0, size // tile, body, 0)
        half = c if i == 0 else 1 - c
        rows = pl.ds(pl.multiple_of(half * HALF + lo, 16), size)
        stores.append(
            pltpu.make_async_copy(buf.at[pl.ds(i * HALF + lo, size)], out_ref.at[rows], sems.at[k])
        )
        stores[-1].start()
    arrived = arrived_ref[FF:, :128].astype(F32)
    weight_out[0] = 0.5 * (weight_ref[0] + arrived[0, 0])
    for copy in stores:
        copy.wait()


def shape(*dims, dtype=BF):
    return jax.ShapeDtypeStruct(dims, dtype)


def added(*terms):
    total = terms[0].astype(F32)
    for term in terms[1:]:
        total = total + term.astype(F32)
    return total.astype(BF)


def gather(other, mine, both, own, cot_sent):
    low_a = move(mine, UP, "upA")
    b = move(other, CORE, "B")
    high_b = move(b, DOWN, "downB")
    low_b = move(b, UP, "upB")
    high_a = move(after(mine, b), DOWN, "downA")
    oth = move(after(own, b), CORE, "tokens")
    over = move(lax.dynamic_update_slice(both, b[None], (1, 0, 0)), ACROSS, "across")
    two_a = move(low_a, UP, "twoA")
    two_b = move(high_b, DOWN, "twoB")
    cot_oth = move(after(cot_sent, oth), CORE, "cotangent")
    over_late = after(over, oth, cot_oth, low_b, high_a)
    over_low = move(over_late, UP, "upX")
    over_high = move(over_late, DOWN, "downX")
    over_two_a = move(two_a, ACROSS, "across2A")
    over_two_b = move(two_b, ACROSS, "across2B")
    have = [
        [mine, b, low_a, low_b, high_a, high_b],
        [over, two_a, two_b],
        [over_low, over_high, over_two_a, over_two_b],
    ]
    return oth, cot_oth, have


def scattered(pieces):
    cross_low = move(pieces[1, 1], UP, "upX")
    cross_high = move(pieces[1, -1], DOWN, "downX")
    far = move(pieces[1, 2], ACROSS, "far")
    via_a = move(added(pieces[0, 2][0], far[0]), UP, "viaA")
    via_b = move(added(pieces[0, 2][1], far[1]), DOWN, "viaB")
    up_b = move(after(pieces[0, 1][1], cross_low), UP, "upB")
    down_a = move(after(pieces[0, -1][0], cross_high), DOWN, "downA")
    crossed = move(added(pieces[1, 0], cross_low, cross_high), ACROSS, "crossed")
    up_a = move(added(pieces[0, 1][0], via_a), UP, "upA")
    down_b = move(added(pieces[0, -1][1], via_b), DOWN, "downB")
    return pieces[0, 0], up_a, up_b, down_a, down_b, crossed


def later(f, own, oth, slope):
    n = len(LATER)
    out = pl.pallas_call(
        grad_kernel,
        out_shape=[shape(2, HALF, ROWS)] * n,
        in_specs=[SMEM, ANY, ANY, VMEM],
        out_specs=[ANY] * n,
        scratch_shapes=[
            pltpu.VMEM((n, 2 * ROWS, 2 * ROWS), BF),
            pltpu.VMEM((n, 2, HALF, ROWS), BF),
            pltpu.SemaphoreType.DMA((n, 2)),
            pltpu.SemaphoreType.DMA((n,)),
        ],
        compiler_params=PARAMS,
        cost_estimate=pl.CostEstimate(flops=n * HALF * 2**19, bytes_accessed=n * 2**20, transcendentals=0),
        name="grad",
    )(f, own, oth, slope)
    return dict(zip(LATER, out))


def ahead(offset, sent):
    return lax.ppermute(sent, "rep", [((i - offset) % 16, i) for i in range(16)])


def on_device(params, first, second, weight, tokens, cotangent, step):
    f = lax.axis_index("fsdp").astype(jnp.int32).reshape(1)
    step = step.reshape(1)
    params, first, second = (a[0].T for a in (params, first, second))
    own, cot = tokens[0], cotangent[0].T
    other, mine, both = pl.pallas_call(
        cast_kernel,
        out_shape=[shape(HALF, ROWS), shape(HALF, ROWS), shape(2, HALF, ROWS)],
        in_specs=[SMEM, SMEM, VMEM],
        out_specs=[VMEM] * 3,
        compiler_params=PARAMS,
        name="cast",
    )(f, weight, params)
    cot_sent = lax.dynamic_slice(cot, ((1 - (f[0] & 1)) * HALF, 0), (HALF, ROWS))
    oth, cot_oth, have = gather(other, mine, both, own, cot_sent)

    def stage(k, kernel, specs, *more, outs=0, extra=()):
        n = len(STAGES[k][0])
        return pl.pallas_call(
            kernel,
            out_shape=[shape(HALF, 2 * ROWS, dtype=BF if outs else F32)] + [shape(2, HALF, ROWS)] * outs,
            in_specs=[SMEM, ANY, ANY] + specs + [ANY] * len(have[k]),
            out_specs=[VMEM] + [ANY] * outs,
            scratch_shapes=[
                pltpu.VMEM((max(n, outs), 2 * ROWS, 2 * ROWS), BF),
                pltpu.VMEM((n, HALF, 2 * ROWS), BF),
                pltpu.SemaphoreType.DMA((max(n, outs), 4)),
            ]
            + list(extra),
            compiler_params=PARAMS,
            cost_estimate=pl.CostEstimate(
                flops=(n + outs) * HALF * 2**19, bytes_accessed=n * 2**20, transcendentals=0
            ),
            name="gate" + str(k),
        )(f, own, oth, *more, *have[k])

    (total,) = stage(0, partial(stage_kernel, 0), [])
    (total,) = stage(1, partial(stage_kernel, 1), [VMEM], total)
    slope, *soon = stage(
        2, last_kernel, [VMEM, ANY, VMEM], total, cot, cot_oth, outs=len(SOON),
        extra=[
            pltpu.VMEM((HALF, 2 * ROWS), F32),
            pltpu.VMEM((HALF, ROWS), BF),
            pltpu.SemaphoreType.DMA,
            pltpu.VMEM((len(SOON), 2, HALF, ROWS), BF),
            pltpu.SemaphoreType.DMA((len(SOON),)),
        ],
    )
    pieces = dict(zip(SOON, soon))
    pieces.update(later(f, own, oth, slope))
    kept, other = pl.pallas_call(
        total_kernel,
        out_shape=[shape(HALF, ROWS, dtype=F32), shape(HALF, ROWS)],
        in_specs=[VMEM] * 6,
        out_specs=[VMEM] * 2,
        compiler_params=PARAMS,
        cost_estimate=pl.CostEstimate(flops=2**22, bytes_accessed=4 * 2**20, transcendentals=0),
        name="total",
    )(*scattered(pieces))
    swapped = move(other, CORE, "swap")
    sent, new_first, new_second = pl.pallas_call(
        step_kernel,
        out_shape=[shape(FF + 16, ROWS)] + [shape(FF, ROWS, dtype=F32)] * 2,
        in_specs=[SMEM, SMEM, SMEM] + [VMEM] * 5,
        out_specs=[VMEM, ANY, ANY],
        scratch_shapes=[pltpu.VMEM((FF, ROWS), F32)] * 2 + [pltpu.SemaphoreType.DMA((2, 2, 2))],
        compiler_params=PARAMS,
        cost_estimate=pl.CostEstimate(flops=2**24, bytes_accessed=10 * 2**20, transcendentals=0),
        name="step",
    )(f, step, weight, params, first, second, kept, swapped)
    arrived = lax.switch(step[0] & 3, [partial(ahead, 1 << bit) for bit in range(4)], sent)
    mixed, new_weight = pl.pallas_call(
        mix_kernel,
        out_shape=[shape(FF, ROWS, dtype=F32), shape(1, dtype=F32)],
        in_specs=[SMEM, SMEM, VMEM, VMEM],
        out_specs=[ANY, SMEM],
        scratch_shapes=[pltpu.VMEM((FF, ROWS), F32), pltpu.SemaphoreType.DMA((4,))],
        compiler_params=PARAMS,
        name="mix",
    )(f, weight, sent, arrived)
    return mixed.T[None], new_first.T[None], new_second.T[None], new_weight


def solution(mesh):
    block = P("rep", "fsdp", None)
    in_specs = (block, block, block, P("rep"), block, block, P())
    out_specs = (block, block, block, P("rep"))
    return jax.shard_map(
        on_device, mesh=mesh, in_specs=in_specs, out_specs=out_specs, check_vma=False
    )
```

```python
from functools import partial

import jax
import jax.numpy as jnp
import numpy as np
from jax import lax
from jax.experimental import pallas as pl
from jax.experimental.pallas import tpu as pltpu
from jax.sharding import PartitionSpec as P

ANY = pl.BlockSpec(memory_space=pl.ANY)
VMEM = pl.BlockSpec(memory_space=pltpu.VMEM)
SMEM = pl.BlockSpec(memory_space=pltpu.SMEM)
BF = jnp.bfloat16
F32 = jnp.float32
PARAMS = pltpu.CompilerParams(vmem_limit_bytes=18 * 1024 * 1024)

D = 4096
FF = 1376
HALF = FF // 2
ROWS = 256

STAGES = (
    ([(0, 0), (0, -1), (0, 1)], (2, 2, 2)),
    ([(1, 0), (0, 2)], (1, 2)),
    ([(1, -1), (1, 1), (1, 2)], (1, 1, 2)),
)
SOON = [(1, -1), (1, 1), (1, 2)]
LATER = [(0, 2), (0, 1), (0, -1), (1, 0), (0, 0)]


def route(move):
    pairs = []
    for f in range(16):
        x, y, c = move(f // 8, f // 2 % 4, f % 2)
        pairs.append((f, x % 2 * 8 + y % 4 * 2 + c % 2))
    return pairs


CORE = route(lambda x, y, c: (x, y, c + 1))
UP = route(lambda x, y, c: (x, y + 1, c))
DOWN = route(lambda x, y, c: (x, y - 1, c))
TWO = route(lambda x, y, c: (x, y + 2, c))
ACROSS = route(lambda x, y, c: (x + 1, y, c))


def move(block, way, name):
    with jax.named_scope(name):
        return lax.ppermute(block, "fsdp", way)


def after(block, *others):
    return lax.optimization_barrier((block, *others))[0]


def chip(f, piece):
    dx, dy = piece
    return ((f // 8 + dx) & 1) * 4 + ((f // 2 + dy) & 3)


def cast_kernel(f_ref, weight_ref, params_ref, other_ref, mine_ref, both_ref):
    c = f_ref[0] & 1
    weight = weight_ref[0]

    def half(c):
        rows = pl.ds(pl.multiple_of(c * HALF, 16), HALF)
        return (params_ref[rows, :] / weight).astype(BF)

    other_ref[...] = half(1 - c)
    mine = half(c)
    mine_ref[...] = mine
    both_ref[0] = mine


def token_copies(f, pieces, own_ref, oth_ref, buf, sems):
    copies = []
    for i, piece in enumerate(pieces):
        cols = pl.ds(pl.multiple_of(chip(f, piece) * 2 * ROWS, 2 * ROWS), 2 * ROWS)
        copies.append(
            (
                pltpu.make_async_copy(own_ref.at[:, cols], buf.at[i, pl.ds(0, ROWS)], sems.at[i, 0]),
                pltpu.make_async_copy(oth_ref.at[:, cols], buf.at[i, pl.ds(ROWS, ROWS)], sems.at[i, 1]),
            )
        )
    return copies


def gate_sum(
    f, pieces, own_ref, oth_ref, weights, tok, wbuf, sems, start_ref, out_ref, extra=()
):
    c = f & 1
    copies = token_copies(f, pieces, own_ref, oth_ref, tok, sems)
    for i in range(len(pieces)):
        blocks = ()
        for ab in range(2):
            cols = pl.ds(pl.multiple_of((c ^ ab) * ROWS, ROWS), ROWS)
            blocks += (pltpu.make_async_copy(weights[i][ab], wbuf.at[i, :, cols], sems.at[i, 2 + ab]),)
        copies[i] += blocks
    for group in [*copies, *extra]:
        for copy in group:
            copy.start()
    for i, group in enumerate(copies):
        for copy in group:
            copy.wait()
        term = lax.dot_general(
            wbuf[i], tok[i], (((1,), (1,)), ((), ())), preferred_element_type=F32
        )
        if i > 0:
            out_ref[...] += term
        elif start_ref is None:
            out_ref[...] = term
        else:
            out_ref[...] = start_ref[...] + term


def paired(refs, counts):
    out = []
    for count in counts:
        out.append((refs[0].at[0], refs[0].at[1]) if count == 1 else refs[:2])
        refs = refs[count:]
    return out, refs


def stage_kernel(k, f_ref, own_ref, oth_ref, *refs):
    pieces, counts = STAGES[k]
    sum_ref, refs = (refs[0], refs[1:]) if k else (None, refs)
    weights, (out_ref, tok, wbuf, sems) = paired(refs, counts)
    gate_sum(f_ref[0], pieces, own_ref, oth_ref, weights, tok, wbuf, sems, sum_ref, out_ref)


def last_kernel(f_ref, own_ref, oth_ref, sum_ref, cot_ref, cot_oth_ref, *refs):
    pieces, counts = STAGES[-1]
    weights, refs = paired(refs, counts)
    slope_ref, *outs = refs[:4]
    tok, wbuf, sems, gate, cot, cot_sem, res, out_sems = refs[4:]
    f = f_ref[0]
    c = f & 1
    rows = pl.ds(pl.multiple_of(c * HALF, 16), HALF)
    cot_copy = pltpu.make_async_copy(cot_ref.at[rows, :], cot, cot_sem)
    cot_copy.start()
    extra = token_copies(f, SOON, own_ref, oth_ref, tok, sems)[len(pieces) :]
    gate_sum(f, pieces, own_ref, oth_ref, weights, tok, wbuf, sems, sum_ref, gate, extra)
    cot_copy.wait()

    def slopes(start, size):
        rows = pl.ds(pl.multiple_of(start, 16), size)
        done = []
        for half, part in ((0, cot), (1, cot_oth_ref)):
            cols = slice(half * ROWS, half * ROWS + ROWS)
            g = gate[rows, cols]
            sig = 1.0 / (1.0 + jnp.exp(-g))
            done.append((cols, part[rows, :].astype(F32) * sig * (1.0 + g * (1.0 - sig))))
        for cols, slope in done:
            slope_ref[rows, cols] = slope.astype(BF)

    def body(i, carry):
        slopes(i * 48, 48)
        return carry

    lax.fori_loop(0, HALF // 48, body, 0)
    slopes(HALF - 16, 16)
    for pair in extra:
        for copy in pair:
            copy.wait()
    grad_loop(c, slope_ref, tok, res, outs, out_sems, None)


def grad_loop(c, slope_ref, tok, res, outs, out_sems, arrival):
    def write(i):
        return pltpu.make_async_copy(res.at[i], outs[i], out_sems.at[i])

    def body(i, carry):
        if arrival is not None:
            arrival(i)
        both = jnp.dot(slope_ref[...], tok[i], preferred_element_type=F32).astype(BF)
        for core in range(2):
            res[i, c ^ core] = both[:, core * ROWS : core * ROWS + ROWS]
        for j in range(len(outs)):

            @pl.when(i == j)
            def _():
                write(j).start()

        return carry

    lax.fori_loop(0, len(outs), body, 0)
    for i in range(len(outs)):
        write(i).wait()


def grad_kernel(f_ref, own_ref, oth_ref, slope_ref, *refs):
    n = len(LATER)
    outs, (tok, res, sems, out_sems) = refs[:n], refs[n:]
    f = f_ref[0]
    for pair in token_copies(f, LATER, own_ref, oth_ref, tok, sems):
        for copy in pair:
            copy.start()

    def arrival(i):
        for j, src in enumerate((own_ref, oth_ref)):
            pltpu.make_async_copy(
                src.at[:, pl.ds(0, 2 * ROWS)], tok.at[i, pl.ds(j * ROWS, ROWS)], sems.at[i, j]
            ).wait()

    grad_loop(f & 1, slope_ref, tok, res, outs, out_sems, arrival)


LOG_ONE = np.log(np.float32(0.9))
LOG_TWO = np.log(np.float32(0.999))


def rows_of(c, i, t):
    half = c if i == 0 else 1 - c
    return pl.ds(pl.multiple_of(half * HALF + t * 16, 16), 16)


def total_kernel(base, up_a, up_b, down_a, down_b, crossed, kept_ref, sent_ref):
    def body(t, carry):
        at = pl.ds(pl.multiple_of(t * 16, 16), 16)
        for i, up, down in ((0, up_a, down_a), (1, up_b, down_b)):
            total = base[i, at].astype(F32) + up[at].astype(F32)
            total = total + down[at].astype(F32) + crossed[i, at].astype(F32)
            if i == 0:
                kept_ref[at] = total
            else:
                sent_ref[at] = total.astype(BF)
        return carry

    lax.fori_loop(0, HALF // 16, body, 0)


def grad_rows(kept, swapped, i, at):
    return kept[at] if i == 0 else swapped[at].astype(F32)


def step_kernel(
    f_ref, step_ref, weight_ref, params_ref, first_ref, second_ref, kept, swapped,
    sent_ref, first_out, second_out, first_buf, second_buf, sems,
):
    c = f_ref[0] & 1
    stepf = jnp.full((1, ROWS), step_ref[0], jnp.int32).astype(F32) + 1.0
    rate = 0.01 * jnp.minimum(1.0, stepf / 2000.0)
    corr_one = 1.0 / (1.0 - jnp.exp(stepf * LOG_ONE))
    corr_two = 1.0 / (1.0 - jnp.exp(stepf * LOG_TWO))

    def tile(t):
        at = pl.ds(pl.multiple_of(t * 16, 16), 16)
        done = []
        for i in range(2):
            rows = rows_of(c, i, t)
            grad = grad_rows(kept, swapped, i, at)
            new_first = 0.9 * first_ref[rows] + 0.1 * grad
            new_second = 0.999 * second_ref[rows] + 0.001 * grad * grad
            master = params_ref[rows]
            update = new_first * corr_one / (jnp.sqrt(new_second * corr_two) + 1e-08)
            done.append((i, t, master - rate * (update + 0.1 * master), new_first, new_second))
        return done

    def store(done):
        for i, t, moved, new_first, new_second in done:
            at = pl.ds(pl.multiple_of(i * HALF + t * 16, 16), 16)
            sent_ref[at] = moved.astype(BF)
            first_buf[at] = new_first
            second_buf[at] = new_second

    def body(t, carry):
        store(tile(3 * t) + tile(3 * t + 1) + tile(3 * t + 2))
        return carry

    copies = []
    for k, (lo, size) in enumerate(((0, 336), (336, 336))):
        lax.fori_loop(lo // 48, (lo + size) // 48, body, 0)
        if k == 1:
            store(tile(HALF // 16 - 1))
            size += 16
        for i in range(2):
            half = c if i == 0 else 1 - c
            rows = pl.ds(pl.multiple_of(half * HALF + lo, 16), size)
            at = pl.ds(i * HALF + lo, size)
            for j, (buf, out) in enumerate(((first_buf, first_out), (second_buf, second_out))):
                copies.append(pltpu.make_async_copy(buf.at[at], out.at[rows], sems.at[k, i, j]))
                copies[-1].start()
    sent_ref[FF:] = jnp.full((16, ROWS), weight_ref[0], F32).astype(BF)
    for copy in copies:
        copy.wait()


def mix_kernel(f_ref, weight_ref, sent_ref, arrived_ref, out_ref, weight_out, buf, sems):
    c = f_ref[0] & 1
    stores = []
    for k, (i, lo, size, tile) in enumerate(
        (i, *part) for part in ((0, 352, 176), (352, 336, 112)) for i in range(2)
    ):

        def body(t, carry):
            at = pl.ds(pl.multiple_of(i * HALF + lo + t * tile, 16), tile)
            buf[at] = 0.5 * (sent_ref[at].astype(F32) + arrived_ref[at].astype(F32))
            return carry

        lax.fori_loop(0, size // tile, body, 0)
        half = c if i == 0 else 1 - c
        rows = pl.ds(pl.multiple_of(half * HALF + lo, 16), size)
        stores.append(
            pltpu.make_async_copy(buf.at[pl.ds(i * HALF + lo, size)], out_ref.at[rows], sems.at[k])
        )
        stores[-1].start()
    arrived = arrived_ref[FF:, :128].astype(F32)
    weight_out[0] = 0.5 * (weight_ref[0] + arrived[0, 0])
    for copy in stores:
        copy.wait()


def shape(*dims, dtype=BF):
    return jax.ShapeDtypeStruct(dims, dtype)


def added(*terms):
    total = terms[0].astype(F32)
    for term in terms[1:]:
        total = total + term.astype(F32)
    return total.astype(BF)


def gather(other, mine, both, own, cot_sent):
    low_a = move(mine, UP, "upA")
    b = move(other, CORE, "B")
    high_b = move(b, DOWN, "downB")
    low_b = move(b, UP, "upB")
    high_a = move(after(mine, b), DOWN, "downA")
    oth = move(after(own, b), CORE, "tokens")
    over = move(lax.dynamic_update_slice(both, b[None], (1, 0, 0)), ACROSS, "across")
    two_a = move(low_a, UP, "twoA")
    two_b = move(high_b, DOWN, "twoB")
    cot_oth = move(after(cot_sent, oth), CORE, "cotangent")
    over_late = after(over, oth, cot_oth, low_b, high_a)
    over_low = move(over_late, UP, "upX")
    over_high = move(over_late, DOWN, "downX")
    over_two_a = move(two_a, ACROSS, "across2A")
    over_two_b = move(two_b, ACROSS, "across2B")
    have = [
        [mine, b, low_a, low_b, high_a, high_b],
        [over, two_a, two_b],
        [over_low, over_high, over_two_a, over_two_b],
    ]
    return oth, cot_oth, have


def scattered(pieces):
    cross_low = move(pieces[1, 1], UP, "upX")
    cross_high = move(pieces[1, -1], DOWN, "downX")
    far = move(pieces[1, 2], ACROSS, "far")
    via_a = move(added(pieces[0, 2][0], far[0]), UP, "viaA")
    via_b = move(added(pieces[0, 2][1], far[1]), DOWN, "viaB")
    up_b = move(pieces[0, 1][1], UP, "upB")
    down_a = move(pieces[0, -1][0], DOWN, "downA")
    crossed = move(added(pieces[1, 0], cross_low, cross_high), ACROSS, "crossed")
    up_a = move(added(pieces[0, 1][0], via_a), UP, "upA")
    down_b = move(added(pieces[0, -1][1], via_b), DOWN, "downB")
    return pieces[0, 0], up_a, up_b, down_a, down_b, crossed


def later(f, own, oth, slope):
    n = len(LATER)
    out = pl.pallas_call(
        grad_kernel,
        out_shape=[shape(2, HALF, ROWS)] * n,
        in_specs=[SMEM, ANY, ANY, VMEM],
        out_specs=[ANY] * n,
        scratch_shapes=[
            pltpu.VMEM((n, 2 * ROWS, 2 * ROWS), BF),
            pltpu.VMEM((n, 2, HALF, ROWS), BF),
            pltpu.SemaphoreType.DMA((n, 2)),
            pltpu.SemaphoreType.DMA((n,)),
        ],
        compiler_params=PARAMS,
        cost_estimate=pl.CostEstimate(flops=n * HALF * 2**19, bytes_accessed=n * 2**20, transcendentals=0),
        name="grad",
    )(f, own, oth, slope)
    return dict(zip(LATER, out))


def ahead(offset, sent):
    return lax.ppermute(sent, "rep", [((i - offset) % 16, i) for i in range(16)])


def on_device(params, first, second, weight, tokens, cotangent, step):
    f = lax.axis_index("fsdp").astype(jnp.int32).reshape(1)
    step = step.reshape(1)
    params, first, second = (a[0].T for a in (params, first, second))
    own, cot = tokens[0], cotangent[0].T
    other, mine, both = pl.pallas_call(
        cast_kernel,
        out_shape=[shape(HALF, ROWS), shape(HALF, ROWS), shape(2, HALF, ROWS)],
        in_specs=[SMEM, SMEM, VMEM],
        out_specs=[VMEM] * 3,
        compiler_params=PARAMS,
        name="cast",
    )(f, weight, params)
    cot_sent = lax.dynamic_slice(cot, ((1 - (f[0] & 1)) * HALF, 0), (HALF, ROWS))
    oth, cot_oth, have = gather(other, mine, both, own, cot_sent)

    def stage(k, kernel, specs, *more, outs=0, extra=()):
        n = len(STAGES[k][0])
        return pl.pallas_call(
            kernel,
            out_shape=[shape(HALF, 2 * ROWS, dtype=BF if outs else F32)] + [shape(2, HALF, ROWS)] * outs,
            in_specs=[SMEM, ANY, ANY] + specs + [ANY] * len(have[k]),
            out_specs=[VMEM] + [ANY] * outs,
            scratch_shapes=[
                pltpu.VMEM((max(n, outs), 2 * ROWS, 2 * ROWS), BF),
                pltpu.VMEM((n, HALF, 2 * ROWS), BF),
                pltpu.SemaphoreType.DMA((max(n, outs), 4)),
            ]
            + list(extra),
            compiler_params=PARAMS,
            cost_estimate=pl.CostEstimate(
                flops=(n + outs) * HALF * 2**19, bytes_accessed=n * 2**20, transcendentals=0
            ),
            name="gate" + str(k),
        )(f, own, oth, *more, *have[k])

    (total,) = stage(0, partial(stage_kernel, 0), [])
    (total,) = stage(1, partial(stage_kernel, 1), [VMEM], total)
    slope, *soon = stage(
        2, last_kernel, [VMEM, ANY, VMEM], total, cot, cot_oth, outs=len(SOON),
        extra=[
            pltpu.VMEM((HALF, 2 * ROWS), F32),
            pltpu.VMEM((HALF, ROWS), BF),
            pltpu.SemaphoreType.DMA,
            pltpu.VMEM((len(SOON), 2, HALF, ROWS), BF),
            pltpu.SemaphoreType.DMA((len(SOON),)),
        ],
    )
    pieces = dict(zip(SOON, soon))
    pieces.update(later(f, own, oth, slope))
    kept, other = pl.pallas_call(
        total_kernel,
        out_shape=[shape(HALF, ROWS, dtype=F32), shape(HALF, ROWS)],
        in_specs=[VMEM] * 6,
        out_specs=[VMEM] * 2,
        compiler_params=PARAMS,
        cost_estimate=pl.CostEstimate(flops=2**22, bytes_accessed=4 * 2**20, transcendentals=0),
        name="total",
    )(*scattered(pieces))
    swapped = move(other, CORE, "swap")
    sent, new_first, new_second = pl.pallas_call(
        step_kernel,
        out_shape=[shape(FF + 16, ROWS)] + [shape(FF, ROWS, dtype=F32)] * 2,
        in_specs=[SMEM, SMEM, SMEM] + [VMEM] * 5,
        out_specs=[VMEM, ANY, ANY],
        scratch_shapes=[pltpu.VMEM((FF, ROWS), F32)] * 2 + [pltpu.SemaphoreType.DMA((2, 2, 2))],
        compiler_params=PARAMS,
        cost_estimate=pl.CostEstimate(flops=2**24, bytes_accessed=10 * 2**20, transcendentals=0),
        name="step",
    )(f, step, weight, params, first, second, kept, swapped)
    arrived = lax.switch(step[0] & 3, [partial(ahead, 1 << bit) for bit in range(4)], sent)
    mixed, new_weight = pl.pallas_call(
        mix_kernel,
        out_shape=[shape(FF, ROWS, dtype=F32), shape(1, dtype=F32)],
        in_specs=[SMEM, SMEM, VMEM, VMEM],
        out_specs=[ANY, SMEM],
        scratch_shapes=[pltpu.VMEM((FF, ROWS), F32), pltpu.SemaphoreType.DMA((4,))],
        compiler_params=PARAMS,
        name="mix",
    )(f, weight, sent, arrived)
    return mixed.T[None], new_first.T[None], new_second.T[None], new_weight


def solution(mesh):
    block = P("rep", "fsdp", None)
    in_specs = (block, block, block, P("rep"), block, block, P())
    out_specs = (block, block, block, P("rep"))
    return jax.shard_map(
        on_device, mesh=mesh, in_specs=in_specs, out_specs=out_specs, check_vma=False
    )
```
